512 devices in a mesh: sgroup: 32 (over z_lo, y), tile: 16 (over x, z_hi, core).
Axes of the slice: x: 4, y: 4, z: 16 (z_hi: 2, z_lo: 8; z = z_hi * 8 + z_lo), core: 2. Of those that a mesh axis runs over, the one named last changes fastest.
Arguments:
- voltages: bfloat16 [2, 512, 256, 2, 16, 128], P(None, 'sgroup', 'tile'), may hold values from -6 to 6
- weights: bfloat16 [2, 512, 256, 2, 16], P(None, 'sgroup'), may hold values from -0.25 to 0.25
- antenna_slot_index: int32 [512, 256], P('sgroup', 'tile'), may hold values from 0 to 255, each once within a row
- station_order: int32 [512], replicated, may hold values from 0 to 511, each once
Outputs:
- visibilities: float32 [16, 2, 1024, 1024], P('tile', None, 'sgroup')
The draws below stay inside these ranges and needn't reach their ends.
Inputs may be any that keep to these rules, and one draw needn't show every extreme that they name: `station_order`: each station slot holds a different station. `antenna_slot_index`: within each station slot, each antenna slot holds a different antenna.
All inputs are finite; a program needn't handle non-finite values.
Results may differ from the reference program's by a relative error of at most 0.0038.
Values may be sent and summed in bfloat16 or wider, within the bound.
A program may use at most 64 MiB of HBM per device.

```python
import jax
import jax.numpy as jnp
from jax import lax

ANTENNA_COUNT = 256
POLAR_COUNT = 2
CHANNEL_COUNT = 16
SPECTRA_COUNT = 128
STATION_COUNT = 512


def level_of(rng, extent, pieces, low, high):
    factor_of, own = 1.0, jax.random.fold_in(rng, 6)
    for position, blocks in pieces:
        heights = jnp.exp(jax.random.uniform(jax.random.fold_in(own, position), (blocks,), jnp.float32, low / len(pieces), high / len(pieces)))
        factor_of = factor_of * jnp.repeat(heights, extent[position] // blocks).reshape([-1 if axis == position else 1 for axis in range(len(extent))])
    return factor_of


def bell_draw(stream_key, dims, width, bound, cuts=(), held_as=jnp.bfloat16):
    entries = jax.random.normal(stream_key, dims, jnp.float32) * width
    if len(cuts) > 0:
        entries = level_of(stream_key, dims, cuts, -0.22, 0.18) * entries
    return jnp.clip(entries, min=-bound, max=bound).astype(held_as)


def setup_inputs(seed: int = 0) -> dict:
    key_list = jax.random.split(jax.random.key(seed), 5)
    return {
        "voltages": bell_draw(key_list[0], (2, STATION_COUNT, ANTENNA_COUNT, POLAR_COUNT, CHANNEL_COUNT, SPECTRA_COUNT), 1.0, 6.0, ((1, 32), (2, 16))),
        "weights": bell_draw(key_list[1], (2, STATION_COUNT, ANTENNA_COUNT, POLAR_COUNT, CHANNEL_COUNT), (2 * ANTENNA_COUNT) ** -0.5, 0.25, ((1, 32),)),
        "antenna_slot_index": jax.vmap(lambda own: jax.random.permutation(own, ANTENNA_COUNT))(jax.random.split(key_list[2], STATION_COUNT)).reshape((STATION_COUNT, ANTENNA_COUNT)).astype(jnp.int32),
        "station_order": jax.random.permutation(key_list[3], STATION_COUNT).astype(jnp.int32),
    }


def reference(voltages, weights, antenna_slot_index, station_order):
    stations = voltages.shape[1]
    slots = jnp.arange(stations, dtype=jnp.int32)[:, None]
    chosen = weights[:, slots, antenna_slot_index].astype(jnp.float32)

    def station_beam(index):
        volt = voltages[:, index].astype(jnp.float32)
        wsel = chosen[:, index]
        real_part = jnp.einsum("apc,apct->cpt", wsel[0], volt[0]) - jnp.einsum("apc,apct->cpt", wsel[1], volt[1])
        imag_part = jnp.einsum("apc,apct->cpt", wsel[0], volt[1]) + jnp.einsum("apc,apct->cpt", wsel[1], volt[0])
        return jnp.stack([real_part, imag_part], axis=1)

    stacked = lax.map(station_beam, jnp.arange(stations, dtype=jnp.int32))
    beams = jnp.transpose(stacked, (1, 2, 0, 3, 4)).astype(jnp.bfloat16)
    ordered = jnp.zeros_like(beams).at[:, :, station_order].set(beams)
    channels, _, _, polars, spectra = ordered.shape
    every_row = ordered.reshape(channels, 2, stations * polars, spectra)
    scale = 1.0 / spectra

    def correlate(block):
        real_in = block[0]
        imag_in = block[1]
        visibility_real = jnp.dot(real_in, real_in.T, preferred_element_type=jnp.float32) + jnp.dot(imag_in, imag_in.T, preferred_element_type=jnp.float32)
        imag_vis = jnp.dot(imag_in, real_in.T, preferred_element_type=jnp.float32) - jnp.dot(real_in, imag_in.T, preferred_element_type=jnp.float32)
        return jnp.stack([visibility_real * scale, imag_vis * scale], axis=0)

    return lax.map(correlate, every_row)
```

```python
import functools

import jax
import jax.numpy as jnp
from jax import lax
from jax.experimental import pallas as pl
from jax.experimental.pallas import tpu as pltpu
from jax.sharding import PartitionSpec as P

MESH = pl.DeviceIdType.MESH
F32, BF16, I32 = jnp.float32, jnp.bfloat16, jnp.int32
X_TYPE, Z_TYPE = BF16, F32
STATIONS, SLOTS, POLARS, CHANNELS, SPECTRA, ANTENNAS = 16, 16, 2, 16, 128, 256


def iota(shape, dim):
    return lax.broadcasted_iota(I32, shape, dim)


def as_bf16(mask):
    return jnp.where(mask, 1.0, 0.0).astype(BF16)


def kernel(
    volt, wt, idx_in, order_in, out,
    idx, order, vbuf, wbuf, wexp, part, core_in, x_out, x_in, z_own, z_out, z_in, held, perm, ordered,
    i_sem, v_sem, w_sem, core_s, core_r, x_s, x_r, zi_s, zi_r, z1_s, z1_r, z2_s, z2_r, y_s, y_r, f_s, f_r,
):
    group, tile = lax.axis_index("sgroup"), lax.axis_index("tile")
    zh4, zq, y = group // 16, (group // 4) % 4, group % 4
    x, zi, core = tile // 4, (tile // 2) % 2, tile % 2

    def at(g, t):
        return {"sgroup": g, "tile": t}

    sibling = at(group, x * 4 + zi * 2 + (1 - core))
    x_peer = [at(group, ((x + d) % 4) * 4 + zi * 2 + core) for d in (1, 2, 3)]
    zi_peer = at(group, x * 4 + (1 - zi) * 2 + core)
    z1_peer = at((1 - zh4) * 16 + zq * 4 + y, tile)
    z2_peer = [at(zh4 * 16 + ((zq + d) % 4) * 4 + y, tile) for d in (1, 2, 3)]
    y_next, y_last = (y + 1) % 4, (y + 3) % 4
    y_peer = [at(zh4 * 16 + zq * 4 + y_next, tile), at(zh4 * 16 + zq * 4 + y_last, tile)]

    barrier = pltpu.get_barrier_semaphore()
    partners = [sibling, *x_peer, zi_peer, z1_peer, *z2_peer, *y_peer]

    small = [
        pltpu.make_async_copy(idx_in, idx, i_sem.at[0]),
        pltpu.make_async_copy(order_in, order, i_sem.at[1]),
    ]
    for copy in small:
        copy.start()
    w_copy = pltpu.make_async_copy(wt, wbuf, w_sem)
    w_copy.start()
    v_copies = []
    for p in range(POLARS):
        for q in range(2):
            copy = pltpu.make_async_copy(
                volt.at[:, pl.ds(q * 8, 8), :, p], vbuf.at[p, :, pl.ds(q * 8, 8)], v_sem.at[p, q]
            )
            copy.start()
            v_copies.append(copy)

    for partner in partners:
        pl.semaphore_signal(barrier, inc=1, device_id=partner, device_id_type=MESH)
    pl.semaphore_wait(barrier, len(partners))

    started = []

    def send(src, dst, s, r, device):
        copy = pltpu.make_async_remote_copy(
            src_ref=src, dst_ref=dst, send_sem=s, recv_sem=r, device_id=device, device_id_type=MESH
        )
        copy.start()
        started.append(copy)

    def arrived(dst, s, r):
        pltpu.make_async_remote_copy(
            src_ref=dst, dst_ref=dst, send_sem=s, recv_sem=r, device_id=sibling, device_id_type=MESH
        ).wait_recv()

    for copy in small:
        copy.wait()
    lanes = SLOTS * CHANNELS
    spread = as_bf16(iota((SLOTS, lanes), 0) == iota((SLOTS, lanes), 1) % SLOTS)
    wide = jnp.dot(idx[...].astype(BF16), spread, preferred_element_type=F32)
    own_lane = iota((STATIONS, lanes), 0) == iota((STATIONS, lanes), 1) // SLOTS
    wide = jnp.where(own_lane, wide, 0.0).astype(BF16)
    number = jnp.dot(jnp.ones((ANTENNAS, STATIONS), BF16), wide, preferred_element_type=F32)
    onehot = as_bf16(number == iota((ANTENNAS, lanes), 0).astype(F32))
    unfold = as_bf16(iota((lanes, lanes), 0) % SLOTS == iota((lanes, lanes), 1) // CHANNELS)
    w_copy.wait()

    def pick(step, carry):
        kept = (step % 2) * 8 + iota((256, lanes), 0) // 32 == iota((256, lanes), 1) // SLOTS
        block = wbuf[pl.ds(pl.multiple_of(step * 256, 256), 256), :]
        got = jnp.dot(block, onehot, preferred_element_type=F32)
        got = jnp.where(kept, got, 0.0).astype(BF16)
        got = jnp.dot(got, unfold, preferred_element_type=F32)
        same = iota((256, lanes), 0) % CHANNELS == iota((256, lanes), 1) % CHANNELS
        wexp[pl.ds(pl.multiple_of(step * 256, 256), 256), :] = jnp.where(same, got, 0.0).astype(BF16)
        return carry

    lax.fori_loop(0, 4, pick, 0)

    slabs = part.reshape(POLARS, 4, 2, 2, 2, STATIONS, SPECTRA)
    for p in range(POLARS):
        for q in range(2):
            v_copies[p * 2 + q].wait()
            for s in range(q * 8, q * 8 + 8):
                left = jnp.concatenate(
                    [wexp[pl.ds(((k * STATIONS + s) * 2 + p) * 16, 16), :] for k in (0, 1)], axis=0
                )
                right = jnp.concatenate(
                    [vbuf[p, k, s].reshape(lanes, SPECTRA) for k in (0, 1)], axis=1
                )
                both = jnp.dot(left, right, preferred_element_type=F32)
                real = both[:16, :SPECTRA] - both[16:, SPECTRA:]
                imag = both[:16, SPECTRA:] + both[16:, :SPECTRA]
                part[pl.ds(p * 512 + s, 16, stride=32), :] = real
                part[pl.ds(p * 512 + 16 + s, 16, stride=32), :] = imag
        send(slabs.at[p, :, :, 1 - core], core_in.at[p], core_s.at[p], core_r.at[p], sibling)

    lane_row = jnp.concatenate([order[...] * 2, order[...] * 2 + 1], axis=1)

    def fill(step, carry):
        rows = step * 64 + iota((64, 1024), 0)
        perm[pl.ds(pl.multiple_of(step * 64, 64), 64), :] = as_bf16(rows == lane_row)
        return carry

    lax.fori_loop(0, 4, fill, 0)
    for p in range(POLARS):
        arrived(core_in.at[p], core_s.at[p], core_r.at[p])
        for d in (1, 2, 3):
            to = (x + d) % 4
            x_out[p, d - 1] = (slabs[p, to, :, core] + core_in[p, to]).astype(X_TYPE)
            send(x_out.at[p, d - 1], x_in.at[p, d - 1], x_s.at[p, d - 1], x_r.at[p, d - 1], x_peer[d - 1])
    lax.fori_loop(4, 8, fill, 0)
    for p in range(POLARS):
        total = slabs[p, x, :, core] + core_in[p, x]
        for d in (1, 2, 3):
            arrived(x_in.at[p, d - 1], x_s.at[p, d - 1], x_r.at[p, d - 1])
            total += x_in[p, d - 1].astype(F32)
        z_own[p] = total
        z_out[p] = z_own[p, 1 - zi].astype(Z_TYPE)
        send(z_out.at[p], z_in.at[p], zi_s.at[p], zi_r.at[p], zi_peer)
    lax.fori_loop(8, 16, fill, 0)
    for p in range(POLARS):
        arrived(z_in.at[p], zi_s.at[p], zi_r.at[p])
        held[zh4, zq, y, p] = (z_own[p, zi] + z_in[p].astype(F32)).astype(BF16)
        mine = held.at[zh4, zq, y, p]
        send(mine, mine, z1_s.at[p], z1_r.at[p], z1_peer)

    def to_y(p, d):
        both = held.at[:, (zq - d + 4) % 4, y, p]
        for way in range(2):
            send(both, both, y_s.at[way, d, p], y_r.at[way, d, p], y_peer[way])

    def forward(p, d):
        for way, source in enumerate((y_last, y_next)):
            got = held.at[:, (zq - d + 4) % 4, source, p]
            arrived(got, y_s.at[way, d, p], y_r.at[way, d, p])
            half = held.at[:, (zq - d + 4) % 4, source, p, way]
            send(half, half, f_s.at[way, d, p], f_r.at[way, d, p], y_peer[way])

    for p in range(POLARS):
        theirs = held.at[1 - zh4, zq, y, p]
        arrived(theirs, z1_s.at[p], z1_r.at[p])
        both = held.at[:, zq, y, p]
        for d in (1, 2, 3):
            send(both, both, z2_s.at[d - 1, p], z2_r.at[d - 1, p], z2_peer[d - 1])
        to_y(p, 0)
    for d in (1, 2, 3):
        for p in range(POLARS):
            arrived(held.at[:, (zq - d + 4) % 4, y, p], z2_s.at[d - 1, p], z2_r.at[d - 1, p])
            to_y(p, d)
        for p in range(POLARS):
            forward(p, d - 1)
    for p in range(POLARS):
        forward(p, 3)
    y_far = (y + 2) % 4
    for d in range(4):
        for p in range(POLARS):
            for way in range(2):
                half = held.at[:, (zq - d + 4) % 4, y_far, p, way]
                arrived(half, f_s.at[way, d, p], f_r.at[way, d, p])

    right = jnp.concatenate(
        [
            jnp.concatenate([held[:, :, :, p, k].reshape(512, SPECTRA) for p in range(POLARS)], axis=0)
            for k in range(2)
        ],
        axis=1,
    )

    def arrange(step, carry):
        rows = pl.ds(pl.multiple_of(step * 256, 256), 256)
        ordered[rows, :] = jnp.dot(perm[rows, :], right, preferred_element_type=F32).astype(BF16)
        return carry

    lax.fori_loop(0, 4, arrange, 0)
    mine = ordered[pl.ds(pl.multiple_of(group * 32, 32), 32), :]
    turned = jnp.concatenate([mine[:, SPECTRA:], -mine[:, :SPECTRA]], axis=1)
    left = jnp.concatenate([mine, turned], axis=0)
    for step in range(4):
        block = ordered[pl.ds(step * 256, 256), :]
        seen = lax.dot_general(left, block, (((1,), (1,)), ((), ())), preferred_element_type=F32)
        seen = seen * (1.0 / SPECTRA)
        out[0, :, pl.ds(step * 256, 256)] = seen[:32]
        out[1, :, pl.ds(step * 256, 256)] = seen[32:]
    for copy in started:
        copy.wait_send()


def body(voltages, weights, antenna_slot_index, station_order):
    wt = jnp.transpose(weights, (0, 1, 3, 4, 2)).reshape(1024, ANTENNAS)
    vmem = pl.BlockSpec(memory_space=pltpu.VMEM)
    hbm = pl.BlockSpec(memory_space=pltpu.HBM)
    sem = pltpu.SemaphoreType.DMA
    out = pl.pallas_call(
        kernel,
        out_shape=jax.ShapeDtypeStruct((2, 32, 1024), F32),
        in_specs=[hbm, hbm, hbm, hbm],
        out_specs=vmem,
        scratch_shapes=[
            pltpu.VMEM((STATIONS, SLOTS), I32),
            pltpu.VMEM((1, 512), I32),
            pltpu.VMEM((2, 2, STATIONS, SLOTS, CHANNELS, SPECTRA), BF16),
            pltpu.VMEM((1024, ANTENNAS), BF16),
            pltpu.VMEM((1024, 256), BF16),
            pltpu.VMEM((1024, SPECTRA), F32),
            pltpu.VMEM((2, 4, 2, 2, STATIONS, SPECTRA), F32),
            pltpu.VMEM((2, 3, 2, 2, STATIONS, SPECTRA), X_TYPE),
            pltpu.VMEM((2, 3, 2, 2, STATIONS, SPECTRA), X_TYPE),
            pltpu.VMEM((2, 2, 2, STATIONS, SPECTRA), F32),
            pltpu.VMEM((2, 2, STATIONS, SPECTRA), Z_TYPE),
            pltpu.VMEM((2, 2, STATIONS, SPECTRA), Z_TYPE),
            pltpu.VMEM((2, 4, 4, 2, 2, STATIONS, SPECTRA), BF16),
            pltpu.VMEM((1024, 1024), BF16),
            pltpu.VMEM((1024, 256), BF16),
            sem((2,)), sem((2, 2)), sem,
            sem((2,)), sem((2,)),
            sem((2, 3)), sem((2, 3)),
            sem((2,)), sem((2,)),
            sem((2,)), sem((2,)),
            sem((3, 2)), sem((3, 2)),
            sem((2, 4, 2)), sem((2, 4, 2)),
            sem((2, 4, 2)), sem((2, 4, 2)),
        ],
        compiler_params=pltpu.CompilerParams(
            collective_id=0, has_side_effects=True, vmem_limit_bytes=56 * 2**20
        ),
    )(voltages, wt, antenna_slot_index, station_order.reshape(1, 512))
    return out[None]


def solution(mesh):
    in_specs = (
        P(None, "sgroup", "tile", None, None, None),
        P(None, "sgroup", None, None, None),
        P("sgroup", "tile"),
        P(),
    )
    out_specs = P("tile", None, "sgroup", None)
    return jax.shard_map(body, mesh=mesh, in_specs=in_specs, out_specs=out_specs, check_vma=False)
```

```python
import functools

import jax
import jax.numpy as jnp
from jax import lax
from jax.experimental import pallas as pl
from jax.experimental.pallas import tpu as pltpu
from jax.sharding import PartitionSpec as P

MESH = pl.DeviceIdType.MESH
F32, BF16, I32 = jnp.float32, jnp.bfloat16, jnp.int32
X_TYPE = F32
STATIONS, SLOTS, POLARS, CHANNELS, SPECTRA, ANTENNAS = 16, 16, 2, 16, 128, 256


def iota(shape, dim):
    return lax.broadcasted_iota(I32, shape, dim)


def as_bf16(mask):
    return jnp.where(mask, 1.0, 0.0).astype(BF16)


def kernel(
    volt, wt, idx_in, order_in, out,
    idx, order, vbuf, wbuf, wexp, part, core_in, x_out, x_in, z_own, z_out, z_in, held, perm, ordered,
    i_sem, v_sem, w_sem, core_s, core_r, x_s, x_r, zi_s, zi_r, y_s, y_r,
):
    group, tile = lax.axis_index("sgroup"), lax.axis_index("tile")
    z, y = group // 4, group % 4
    zh, par = z // 2, z % 2
    x, zi, core = tile // 4, (tile // 2) % 2, tile % 2

    def at(g, t):
        return {"sgroup": g, "tile": t}

    sibling = at(group, x * 4 + zi * 2 + (1 - core))
    x_peer = [at(group, ((x + d) % 4) * 4 + zi * 2 + core) for d in (1, 2, 3)]
    z_steps = [(1, 0), (0, 2), (1, 2), (0, 1), (1, 1), (0, 3), (1, 3)]
    half_of = (zi, 1 - zi)
    z_peer = [
        at((((zh + d) % 4) * 2 + par) * 4 + y, x * 4 + half_of[h] * 2 + core) for h, d in z_steps
    ]
    y_steps = [(1, 0), (0, 1), (0, 3), (0, 2), (1, 1), (1, 3), (1, 2)]
    par_of = (par, 1 - par)
    y_peer = [at((zh * 2 + par_of[h]) * 4 + (y + d) % 4, tile) for h, d in y_steps]

    barrier = pltpu.get_barrier_semaphore()
    partners = [sibling, *x_peer, *z_peer, *y_peer]

    small = [
        pltpu.make_async_copy(idx_in, idx, i_sem.at[0]),
        pltpu.make_async_copy(order_in, order, i_sem.at[1]),
    ]
    for copy in small:
        copy.start()
    w_copy = pltpu.make_async_copy(wt, wbuf, w_sem)
    w_copy.start()
    v_copies = []
    for p in range(POLARS):
        for q in range(2):
            copy = pltpu.make_async_copy(
                volt.at[:, pl.ds(q * 8, 8), :, p], vbuf.at[p, :, pl.ds(q * 8, 8)], v_sem.at[p, q]
            )
            copy.start()
            v_copies.append(copy)

    for partner in partners:
        pl.semaphore_signal(barrier, inc=1, device_id=partner, device_id_type=MESH)

    started = []

    def send(src, dst, s, r, device):
        copy = pltpu.make_async_remote_copy(
            src_ref=src, dst_ref=dst, send_sem=s, recv_sem=r, device_id=device, device_id_type=MESH
        )
        copy.start()
        started.append(copy)

    def arrived(dst, s, r):
        pltpu.make_async_remote_copy(
            src_ref=dst, dst_ref=dst, send_sem=s, recv_sem=r, device_id=sibling, device_id_type=MESH
        ).wait_recv()

    for copy in small:
        copy.wait()
    lanes = SLOTS * CHANNELS
    spread = as_bf16(iota((SLOTS, lanes), 0) == iota((SLOTS, lanes), 1) % SLOTS)
    wide = jnp.dot(idx[...].astype(BF16), spread, preferred_element_type=F32)
    own_lane = iota((STATIONS, lanes), 0) == iota((STATIONS, lanes), 1) // SLOTS
    wide = jnp.where(own_lane, wide, 0.0).astype(BF16)
    number = jnp.dot(jnp.ones((ANTENNAS, STATIONS), BF16), wide, preferred_element_type=F32)
    onehot = as_bf16(number == iota((ANTENNAS, lanes), 0).astype(F32))
    unfold = as_bf16(iota((lanes, lanes), 0) % SLOTS == iota((lanes, lanes), 1) // CHANNELS)
    w_copy.wait()

    def pick(step, carry):
        kept = (step % 2) * 8 + iota((256, lanes), 0) // 32 == iota((256, lanes), 1) // SLOTS
        block = wbuf[pl.ds(pl.multiple_of(step * 256, 256), 256), :]
        got = jnp.dot(block, onehot, preferred_element_type=F32)
        got = jnp.where(kept, got, 0.0).astype(BF16)
        got = jnp.dot(got, unfold, preferred_element_type=F32)
        same = iota((256, lanes), 0) % CHANNELS == iota((256, lanes), 1) % CHANNELS
        wexp[pl.ds(pl.multiple_of(step * 256, 256), 256), :] = jnp.where(same, got, 0.0).astype(BF16)
        return carry

    lax.fori_loop(0, 4, pick, 0)

    pl.semaphore_wait(barrier, len(partners))
    slabs = part.reshape(POLARS, 4, 2, 2, 2, STATIONS, SPECTRA)
    for p in range(POLARS):
        for q in range(2):
            v_copies[p * 2 + q].wait()
            for s in range(q * 8, q * 8 + 8):
                left = jnp.concatenate(
                    [wexp[pl.ds(((k * STATIONS + s) * 2 + p) * 16, 16), :] for k in (0, 1)], axis=0
                )
                right = jnp.concatenate(
                    [vbuf[p, k, s].reshape(lanes, SPECTRA) for k in (0, 1)], axis=1
                )
                both = jnp.dot(left, right, preferred_element_type=F32)
                real = both[:16, :SPECTRA] - both[16:, SPECTRA:]
                imag = both[:16, SPECTRA:] + both[16:, :SPECTRA]
                part[pl.ds(p * 512 + s, 16, stride=32), :] = real
                part[pl.ds(p * 512 + 16 + s, 16, stride=32), :] = imag
        send(slabs.at[p, :, :, 1 - core], core_in.at[p], core_s.at[p], core_r.at[p], sibling)

    lane_row = jnp.concatenate([order[...] * 2, order[...] * 2 + 1], axis=1)

    def fill(step, carry):
        rows = step * 64 + iota((64, 1024), 0)
        perm[pl.ds(pl.multiple_of(step * 64, 64), 64), :] = as_bf16(rows == lane_row)
        return carry

    for p in range(POLARS):
        arrived(core_in.at[p], core_s.at[p], core_r.at[p])
        for d in (1, 2, 3):
            to = (x + d) % 4
            x_out[p, d - 1] = (slabs[p, to, :, core] + core_in[p, to]).astype(X_TYPE)
            send(x_out.at[p, d - 1], x_in.at[p, d - 1], x_s.at[p, d - 1], x_r.at[p, d - 1], x_peer[d - 1])
    lax.fori_loop(0, 8, fill, 0)
    for p in range(POLARS):
        total = slabs[p, x, :, core] + core_in[p, x]
        for d in (1, 2, 3):
            arrived(x_in.at[p, d - 1], x_s.at[p, d - 1], x_r.at[p, d - 1])
            total += x_in[p, d - 1].astype(F32)
        z_own[p] = total
        z_out[p] = total.astype(BF16)
        for j, (h, d) in enumerate(z_steps):
            send(z_out.at[p, half_of[h]], z_in.at[p, h, d], zi_s.at[p, j], zi_r.at[p, j], z_peer[j])
    lax.fori_loop(8, 16, fill, 0)
    for d in (2, 1, 3, 0):
        source = (zh - d + 4) % 4
        for p in range(POLARS):
            for j, (h, step) in enumerate(z_steps):
                if step == d:
                    arrived(z_in.at[p, h, d], zi_s.at[p, j], zi_r.at[p, j])
            first = z_own[p, zi] if d == 0 else z_in[p, 0, d].astype(F32)
            held[source, par, y, p] = (first + z_in[p, 1, d].astype(F32)).astype(BF16)
        mine = held.at[source, par, y]
        for j in range(7):
            send(mine, mine, y_s.at[d, j], y_r.at[d, j], y_peer[j])
    for d in (2, 1, 3, 0):
        source = (zh - d + 4) % 4
        for j, (h, step) in enumerate(y_steps):
            arrived(held.at[source, par_of[h], (y - step + 4) % 4], y_s.at[d, j], y_r.at[d, j])

    right = jnp.concatenate(
        [
            jnp.concatenate([held[:, :, :, p, k].reshape(512, SPECTRA) for p in range(POLARS)], axis=0)
            for k in range(2)
        ],
        axis=1,
    )

    def arrange(step, carry):
        rows = pl.ds(pl.multiple_of(step * 256, 256), 256)
        ordered[rows, :] = jnp.dot(perm[rows, :], right, preferred_element_type=F32).astype(BF16)
        return carry

    lax.fori_loop(0, 4, arrange, 0)
    mine = ordered[pl.ds(pl.multiple_of(group * 32, 32), 32), :]
    turned = jnp.concatenate([mine[:, SPECTRA:], -mine[:, :SPECTRA]], axis=1)
    left = jnp.concatenate([mine, turned], axis=0)
    for step in range(4):
        block = ordered[pl.ds(step * 256, 256), :]
        seen = lax.dot_general(left, block, (((1,), (1,)), ((), ())), preferred_element_type=F32)
        seen = seen * (1.0 / SPECTRA)
        out[0, :, pl.ds(step * 256, 256)] = seen[:32]
        out[1, :, pl.ds(step * 256, 256)] = seen[32:]
    for copy in started:
        copy.wait_send()


def body(voltages, weights, antenna_slot_index, station_order):
    wt = jnp.transpose(weights, (0, 1, 3, 4, 2)).reshape(1024, ANTENNAS)
    vmem = pl.BlockSpec(memory_space=pltpu.VMEM)
    hbm = pl.BlockSpec(memory_space=pltpu.HBM)
    sem = pltpu.SemaphoreType.DMA
    out = pl.pallas_call(
        kernel,
        out_shape=jax.ShapeDtypeStruct((2, 32, 1024), F32),
        in_specs=[hbm, hbm, hbm, hbm],
        out_specs=vmem,
        scratch_shapes=[
            pltpu.VMEM((STATIONS, SLOTS), I32),
            pltpu.VMEM((1, 512), I32),
            pltpu.VMEM((2, 2, STATIONS, SLOTS, CHANNELS, SPECTRA), BF16),
            pltpu.VMEM((1024, ANTENNAS), BF16),
            pltpu.VMEM((1024, 256), BF16),
            pltpu.VMEM((1024, SPECTRA), F32),
            pltpu.VMEM((2, 4, 2, 2, STATIONS, SPECTRA), F32),
            pltpu.VMEM((2, 3, 2, 2, STATIONS, SPECTRA), X_TYPE),
            pltpu.VMEM((2, 3, 2, 2, STATIONS, SPECTRA), X_TYPE),
            pltpu.VMEM((2, 2, 2, STATIONS, SPECTRA), F32),
            pltpu.VMEM((2, 2, 2, STATIONS, SPECTRA), BF16),
            pltpu.VMEM((2, 2, 4, 2, STATIONS, SPECTRA), BF16),
            pltpu.VMEM((4, 2, 4, 2, 2, STATIONS, SPECTRA), BF16),
            pltpu.VMEM((1024, 1024), BF16),
            pltpu.VMEM((1024, 256), BF16),
            sem((2,)), sem((2, 2)), sem,
            sem((2,)), sem((2,)),
            sem((2, 3)), sem((2, 3)),
            sem((2, 7)), sem((2, 7)),
            sem((4, 7)), sem((4, 7)),
        ],
        compiler_params=pltpu.CompilerParams(
            collective_id=0, has_side_effects=True, vmem_limit_bytes=56 * 2**20
        ),
    )(voltages, wt, antenna_slot_index, station_order.reshape(1, 512))
    return out[None]


def solution(mesh):
    in_specs = (
        P(None, "sgroup", "tile", None, None, None),
        P(None, "sgroup", None, None, None),
        P("sgroup", "tile"),
        P(),
    )
    out_specs = P("tile", None, "sgroup", None)
    return jax.shard_map(body, mesh=mesh, in_specs=in_specs, out_specs=out_specs, check_vma=False)
```

```python
import functools

import jax
import jax.numpy as jnp
from jax import lax
from jax.experimental import pallas as pl
from jax.experimental.pallas import tpu as pltpu
from jax.sharding import PartitionSpec as P

MESH = pl.DeviceIdType.MESH
F32, BF16, I32 = jnp.float32, jnp.bfloat16, jnp.int32
STATIONS, SLOTS, POLARS, CHANNELS, SPECTRA, ANTENNAS = 16, 16, 2, 16, 128, 256


def iota(shape, dim):
    return lax.broadcasted_iota(I32, shape, dim)


def as_bf16(mask):
    return jnp.where(mask, 1.0, 0.0).astype(BF16)


def kernel(
    volt, wt, idx_in, order_in, out,
    idx, order, vbuf, wbuf, wexp, part, core_in, x_out, x_in, z_own, z_out, z_in, held, perm, summed, ordered,
    i_sem, v_sem, w_sem, core_s, core_r, x_s, x_r, z_s, z_r, ready, y_s, y_r,
):
    group, tile = lax.axis_index("sgroup"), lax.axis_index("tile")
    z, y = group // 4, group % 4
    zh, par = z // 2, z % 2
    x, zi, core = tile // 4, (tile // 2) % 2, tile % 2

    def at(g, t):
        return {"sgroup": g, "tile": t}

    sibling = at(group, x * 4 + zi * 2 + (1 - core))
    x_peer = [at(group, ((x + d) % 4) * 4 + zi * 2 + core) for d in (1, 2, 3)]
    z_peer = [
        [at((e * 2 + par) * 4 + y, x * 4 + half * 2 + core) for e in range(4)] for half in range(2)
    ]
    near_peer = [at((((zh + d) % 4) * 2 + par) * 4 + y, tile) for d in (1, 2, 3)]
    far_peer = [at((e * 2 + par) * 4 + y, x * 4 + (1 - zi) * 2 + core) for e in range(4)]
    pair_peer = at((zh * 2 + 1 - par) * 4 + y, tile)
    y_steps = [(e, d) for e in (0, 1) for d in (1, 3, 2)]
    y_peer = [at((zh * 2 + e) * 4 + (y + d) % 4, tile) for e, d in y_steps]

    barrier = pltpu.get_barrier_semaphore()
    partners = [sibling, *x_peer, *near_peer, pair_peer, *y_peer]

    small = [
        pltpu.make_async_copy(idx_in, idx, i_sem.at[0]),
        pltpu.make_async_copy(order_in, order, i_sem.at[1]),
    ]
    for copy in small:
        copy.start()
    w_copy = pltpu.make_async_copy(wt, wbuf, w_sem)
    w_copy.start()
    v_copies = []
    for p in range(POLARS):
        for q in range(2):
            copy = pltpu.make_async_copy(
                volt.at[:, pl.ds(q * 8, 8), :, p], vbuf.at[p, :, pl.ds(q * 8, 8)], v_sem.at[p, q]
            )
            copy.start()
            v_copies.append(copy)

    for partner in partners:
        pl.semaphore_signal(barrier, inc=1, device_id=partner, device_id_type=MESH)

    @pl.when(zi == 0)
    def _():
        for partner in far_peer:
            pl.semaphore_signal(barrier, inc=1, device_id=partner, device_id_type=MESH)

    started = []

    def send(src, dst, s, r, device):
        copy = pltpu.make_async_remote_copy(
            src_ref=src, dst_ref=dst, send_sem=s, recv_sem=r, device_id=device, device_id_type=MESH
        )
        copy.start()
        started.append(copy)

    def to_z(h, p, e):
        return pltpu.make_async_remote_copy(
            src_ref=z_out.at[h, p], dst_ref=z_in.at[p, zi, zh], send_sem=z_s.at[h, p, e],
            recv_sem=z_r.at[p, zi, zh], device_id=z_peer[h][e], device_id_type=MESH,
        )

    def arrived(dst, s, r):
        pltpu.make_async_remote_copy(
            src_ref=dst, dst_ref=dst, send_sem=s, recv_sem=r, device_id=sibling, device_id_type=MESH
        ).wait_recv()

    for copy in small:
        copy.wait()
    lanes = SLOTS * CHANNELS
    spread = as_bf16(iota((SLOTS, lanes), 0) == iota((SLOTS, lanes), 1) % SLOTS)
    wide = jnp.dot(idx[...].astype(BF16), spread, preferred_element_type=F32)
    own_lane = iota((STATIONS, lanes), 0) == iota((STATIONS, lanes), 1) // SLOTS
    wide = jnp.where(own_lane, wide, 0.0).astype(BF16)
    number = jnp.dot(jnp.ones((ANTENNAS, STATIONS), BF16), wide, preferred_element_type=F32)
    onehot = as_bf16(number == iota((ANTENNAS, lanes), 0).astype(F32))
    unfold = as_bf16(iota((lanes, lanes), 0) % SLOTS == iota((lanes, lanes), 1) // CHANNELS)
    w_copy.wait()

    def pick(step, carry):
        kept = (step % 2) * 8 + iota((256, lanes), 0) // 32 == iota((256, lanes), 1) // SLOTS
        block = wbuf[pl.ds(pl.multiple_of(step * 256, 256), 256), :]
        got = jnp.dot(block, onehot, preferred_element_type=F32)
        got = jnp.where(kept, got, 0.0).astype(BF16)
        got = jnp.dot(got, unfold, preferred_element_type=F32)
        same = iota((256, lanes), 0) % CHANNELS == iota((256, lanes), 1) % CHANNELS
        wexp[pl.ds(pl.multiple_of(step * 256, 256), 256), :] = jnp.where(same, got, 0.0).astype(BF16)
        return carry

    lax.fori_loop(0, 4, pick, 0)

    pl.semaphore_wait(barrier, len(partners) + 4 * zi)

    @pl.when(zi == 1)
    def _():
        for partner in far_peer:
            pl.semaphore_signal(ready, inc=1, device_id=partner, device_id_type=MESH)

    slabs = part.reshape(POLARS, 4, 2, 2, 2, STATIONS, SPECTRA)
    for p in range(POLARS):
        for q in range(2):
            v_copies[p * 2 + q].wait()
            for s in range(q * 8, q * 8 + 8):
                left = jnp.concatenate(
                    [wexp[pl.ds(((k * STATIONS + s) * 2 + p) * 16, 16), :] for k in (0, 1)], axis=0
                )
                right = jnp.concatenate(
                    [vbuf[p, k, s].reshape(lanes, SPECTRA) for k in (0, 1)], axis=1
                )
                both = jnp.dot(left, right, preferred_element_type=F32)
                real = both[:16, :SPECTRA] - both[16:, SPECTRA:]
                imag = both[:16, SPECTRA:] + both[16:, :SPECTRA]
                part[pl.ds(p * 512 + s, 16, stride=32), :] = real
                part[pl.ds(p * 512 + 16 + s, 16, stride=32), :] = imag
        for h in range(2):
            theirs = slabs.at[p, :, h, 1 - core]
            send(theirs, core_in.at[h, p], core_s.at[h, p], core_r.at[h, p], sibling)

    def fill(step, carry):
        rows = (step % 8) * 128 + iota((128, 256), 0)
        block = order[:, pl.ds(pl.multiple_of((step // 8) * 128, 128), 128)]
        lane_row = jnp.concatenate([block * 2, block * 2 + 1], axis=1)
        perm[step // 8, pl.ds(pl.multiple_of((step % 8) * 128, 128), 128), :] = as_bf16(rows == lane_row)
        return carry

    for h in range(2):
        for p in range(POLARS):
            arrived(core_in.at[h, p], core_s.at[h, p], core_r.at[h, p])
            for d in (1, 2, 3):
                to = (x + d) % 4
                x_out[h, p, d - 1] = slabs[p, to, h, core] + core_in[h, p, to]
                send(
                    x_out.at[h, p, d - 1], x_in.at[h, p, d - 1],
                    x_s.at[h, p, d - 1], x_r.at[h, p, d - 1], x_peer[d - 1],
                )
        lax.fori_loop(h * 16, h * 16 + 16, fill, 0)
        for p in range(POLARS):
            total = slabs[p, x, h, core] + core_in[h, p, x]
            for d in (1, 2, 3):
                arrived(x_in.at[h, p, d - 1], x_s.at[h, p, d - 1], x_r.at[h, p, d - 1])
                total += x_in[h, p, d - 1]
            z_out[h, p] = total.astype(BF16)

            @pl.when(zi == h)
            def _():
                z_own[p] = total

            if h == 1 and p == 0:

                @pl.when(zi == 0)
                def _():
                    pl.semaphore_wait(ready, 4)

            for e in range(4):

                @pl.when(jnp.logical_or(zi != h, zh != e))
                def _():
                    to_z(h, p, e).start()

    for d in (1, 2, 3, 0):
        source = (zh - d + 4) % 4
        for p in range(POLARS):
            if d == 0:
                first = z_own[p]
            else:
                arrived(z_in.at[p, zi, source], z_s.at[0, p, d], z_r.at[p, zi, source])
                first = z_in[p, zi, source].astype(F32)
            arrived(z_in.at[p, 1 - zi, source], z_s.at[1, p, d], z_r.at[p, 1 - zi, source])
            held[source, par, y, p] = (first + z_in[p, 1 - zi, source].astype(F32)).astype(BF16)
        mine = held.at[source, par, y]
        send(mine, mine, y_s.at[d, 6], y_r.at[d, par, 0], pair_peer)
        for j, (_, step) in enumerate(y_steps):
            send(mine, mine, y_s.at[d, j], y_r.at[d, par, step], y_peer[j])

    for d in (1, 2, 3, 0):
        source = (zh - d + 4) % 4
        arrived(held.at[source, 1 - par, y], y_s.at[d, 6], y_r.at[d, 1 - par, 0])
        for j, (e, step) in enumerate(y_steps):
            arrived(held.at[source, e, (y - step + 4) % 4], y_s.at[d, j], y_r.at[d, e, step])
        right = jnp.concatenate(
            [
                jnp.concatenate([held[source, :, :, p, k].reshape(128, SPECTRA) for p in range(POLARS)], axis=0)
                for k in range(2)
            ],
            axis=1,
        )
        for step in range(4):
            rows = pl.ds(step * 256, 256)
            got = jnp.dot(perm[source, rows, :], right, preferred_element_type=F32)
            if d == 1:
                summed[rows, :] = got
            elif d > 0:
                summed[rows, :] += got
            else:
                ordered[rows, :] = (summed[rows, :] + got).astype(BF16)
    mine = ordered[pl.ds(pl.multiple_of(group * 32, 32), 32), :]
    turned = jnp.concatenate([mine[:, SPECTRA:], -mine[:, :SPECTRA]], axis=1)
    left = jnp.concatenate([mine, turned], axis=0)
    for step in range(4):
        block = ordered[pl.ds(step * 256, 256), :]
        seen = lax.dot_general(left, block, (((1,), (1,)), ((), ())), preferred_element_type=F32)
        seen = seen * (1.0 / SPECTRA)
        out[0, :, pl.ds(step * 256, 256)] = seen[:32]
        out[1, :, pl.ds(step * 256, 256)] = seen[32:]
    for copy in started:
        copy.wait_send()
    for h in range(2):
        for p in range(POLARS):
            for e in range(4):

                @pl.when(jnp.logical_or(zi != h, zh != e))
                def _():
                    to_z(h, p, e).wait_send()


def body(voltages, weights, antenna_slot_index, station_order):
    wt = jnp.transpose(weights, (0, 1, 3, 4, 2)).reshape(1024, ANTENNAS)
    vmem = pl.BlockSpec(memory_space=pltpu.VMEM)
    hbm = pl.BlockSpec(memory_space=pltpu.HBM)
    sem = pltpu.SemaphoreType.DMA
    out = pl.pallas_call(
        kernel,
        out_shape=jax.ShapeDtypeStruct((2, 32, 1024), F32),
        in_specs=[hbm, hbm, hbm, hbm],
        out_specs=vmem,
        scratch_shapes=[
            pltpu.VMEM((STATIONS, SLOTS), I32),
            pltpu.VMEM((1, 512), I32),
            pltpu.VMEM((2, 2, STATIONS, SLOTS, CHANNELS, SPECTRA), BF16),
            pltpu.VMEM((1024, ANTENNAS), BF16),
            pltpu.VMEM((1024, 256), BF16),
            pltpu.VMEM((1024, SPECTRA), F32),
            pltpu.VMEM((2, 2, 4, 2, STATIONS, SPECTRA), F32),
            pltpu.VMEM((2, 2, 3, 2, STATIONS, SPECTRA), F32),
            pltpu.VMEM((2, 2, 3, 2, STATIONS, SPECTRA), F32),
            pltpu.VMEM((2, 2, STATIONS, SPECTRA), F32),
            pltpu.VMEM((2, 2, 2, STATIONS, SPECTRA), BF16),
            pltpu.VMEM((2, 2, 4, 2, STATIONS, SPECTRA), BF16),
            pltpu.VMEM((4, 2, 4, 2, 2, STATIONS, SPECTRA), BF16),
            pltpu.VMEM((4, 1024, 256), BF16),
            pltpu.VMEM((1024, 256), F32),
            pltpu.VMEM((1024, 256), BF16),
            sem((2,)), sem((2, 2)), sem,
            sem((2, 2)), sem((2, 2)),
            sem((2, 2, 3)), sem((2, 2, 3)),
            sem((2, 2, 4)), sem((2, 2, 4)), pltpu.SemaphoreType.REGULAR,
            sem((4, 7)), sem((4, 2, 4)),
        ],
        compiler_params=pltpu.CompilerParams(
            collective_id=0, has_side_effects=True, vmem_limit_bytes=56 * 2**20
        ),
    )(voltages, wt, antenna_slot_index, station_order.reshape(1, 512))
    return out[None]


def solution(mesh):
    in_specs = (
        P(None, "sgroup", "tile", None, None, None),
        P(None, "sgroup", None, None, None),
        P("sgroup", "tile"),
        P(),
    )
    out_specs = P("tile", None, "sgroup", None)
    return jax.shard_map(body, mesh=mesh, in_specs=in_specs, out_specs=out_specs, check_vma=False)
```

```python
import functools

import jax
import jax.numpy as jnp
from jax import lax
from jax.experimental import pallas as pl
from jax.experimental.pallas import tpu as pltpu
from jax.sharding import PartitionSpec as P

MESH = pl.DeviceIdType.MESH
F32, BF16, I32 = jnp.float32, jnp.bfloat16, jnp.int32
STATIONS, SLOTS, POLARS, CHANNELS, SPECTRA, ANTENNAS = 16, 16, 2, 16, 128, 256


def iota(shape, dim):
    return lax.broadcasted_iota(I32, shape, dim)


def as_bf16(mask):
    return jnp.where(mask, 1.0, 0.0).astype(BF16)


def kernel(
    volt, wt, idx_in, order_in, out,
    idx, order, vbuf, wbuf, wexp, part, core_in, x_out, x_in, z_own, z_out, near_in, far_in, held, perm, summed, ordered,
    i_sem, v_sem, w_sem, core_s, core_r, x_s, x_r, z_s, z_r, ready, y_s, y_r,
):
    group, tile = lax.axis_index("sgroup"), lax.axis_index("tile")
    z, y = group // 4, group % 4
    zh, par = z // 2, z % 2
    x, zi, core = tile // 4, (tile // 2) % 2, tile % 2

    def at(g, t):
        return {"sgroup": g, "tile": t}

    sibling = at(group, x * 4 + zi * 2 + (1 - core))
    x_peer = [at(group, ((x + d) % 4) * 4 + zi * 2 + core) for d in (1, 2, 3)]
    z_peer = [
        [at((e * 2 + 1 - par) * 4 + y, x * 4 + half * 2 + core) for e in range(4)] for half in (zi, 1 - zi)
    ]
    near_peer, far_peer = z_peer
    pair_peer = at((zh * 2 + 1 - par) * 4 + y, tile)
    y_steps = [(e, d) for e in (0, 1) for d in (1, 3, 2)]
    y_peer = [at((zh * 2 + e) * 4 + (y + d) % 4, tile) for e, d in y_steps]

    barrier = pltpu.get_barrier_semaphore()
    partners = [sibling, *x_peer, pair_peer, *y_peer]

    small = [
        pltpu.make_async_copy(idx_in, idx, i_sem.at[0]),
        pltpu.make_async_copy(order_in, order, i_sem.at[1]),
    ]
    for copy in small:
        copy.start()
    w_copy = pltpu.make_async_copy(wt, wbuf, w_sem)
    w_copy.start()
    v_copies = []
    for p in range(POLARS):
        for q in range(2):
            copy = pltpu.make_async_copy(
                volt.at[:, pl.ds(q * 8, 8), :, p], vbuf.at[p, :, pl.ds(q * 8, 8)], v_sem.at[p, q]
            )
            copy.start()
            v_copies.append(copy)

    for partner in partners:
        pl.semaphore_signal(barrier, inc=1, device_id=partner, device_id_type=MESH)

    @pl.when(zi == 0)
    def _():
        for partner in near_peer + far_peer:
            pl.semaphore_signal(barrier, inc=1, device_id=partner, device_id_type=MESH)

    started = []

    def send(src, dst, s, r, device):
        copy = pltpu.make_async_remote_copy(
            src_ref=src, dst_ref=dst, send_sem=s, recv_sem=r, device_id=device, device_id_type=MESH
        )
        copy.start()
        started.append(copy)

    def to_z(far, e):
        return pltpu.make_async_remote_copy(
            src_ref=(z_own, z_out)[far], dst_ref=(near_in, far_in)[far].at[zh], send_sem=z_s.at[far, e],
            recv_sem=z_r.at[far, zh], device_id=z_peer[far][e], device_id_type=MESH,
        )

    def arrived(dst, s, r):
        pltpu.make_async_remote_copy(
            src_ref=dst, dst_ref=dst, send_sem=s, recv_sem=r, device_id=sibling, device_id_type=MESH
        ).wait_recv()

    for copy in small:
        copy.wait()
    lanes = SLOTS * CHANNELS
    spread = as_bf16(iota((SLOTS, lanes), 0) == iota((SLOTS, lanes), 1) % SLOTS)
    wide = jnp.dot(idx[...].astype(BF16), spread, preferred_element_type=F32)
    own_lane = iota((STATIONS, lanes), 0) == iota((STATIONS, lanes), 1) // SLOTS
    wide = jnp.where(own_lane, wide, 0.0).astype(BF16)
    number = jnp.dot(jnp.ones((ANTENNAS, STATIONS), BF16), wide, preferred_element_type=F32)
    onehot = as_bf16(number == iota((ANTENNAS, lanes), 0).astype(F32))
    unfold = as_bf16(iota((lanes, lanes), 0) % SLOTS == iota((lanes, lanes), 1) // CHANNELS)
    w_copy.wait()

    def pick(step):
        kept = (step % 2) * 8 + iota((256, lanes), 0) // 32 == iota((256, lanes), 1) // SLOTS
        block = wbuf[pl.ds(step * 256, 256), :]
        got = jnp.dot(block, onehot, preferred_element_type=F32)
        got = jnp.where(kept, got, 0.0).astype(BF16)
        got = jnp.dot(got, unfold, preferred_element_type=F32)
        same = iota((256, lanes), 0) % CHANNELS == iota((256, lanes), 1) % CHANNELS
        wexp[pl.ds(step * 256, 256), :] = jnp.where(same, got, 0.0).astype(BF16)

    for step in range(4):
        pick(step)

    pl.semaphore_wait(barrier, len(partners) + 4)

    @pl.when(zi == 1)
    def _():
        for partner in far_peer:
            pl.semaphore_signal(ready, inc=1, device_id=partner, device_id_type=MESH)

    slabs = part.reshape(POLARS, 4, 2, 2, 2, STATIONS, SPECTRA)
    for p in range(POLARS):
        for q in range(2):
            v_copies[p * 2 + q].wait()
            for s in range(q * 8, q * 8 + 8):
                left = jnp.concatenate(
                    [wexp[pl.ds(((k * STATIONS + s) * 2 + p) * 16, 16), :] for k in (0, 1)], axis=0
                )
                right = jnp.concatenate(
                    [vbuf[p, k, s].reshape(lanes, SPECTRA) for k in (0, 1)], axis=1
                )
                both = jnp.dot(left, right, preferred_element_type=F32)
                real = both[:16, :SPECTRA] - both[16:, SPECTRA:]
                imag = both[:16, SPECTRA:] + both[16:, :SPECTRA]
                part[pl.ds(p * 512 + s, 16, stride=32), :] = real
                part[pl.ds(p * 512 + 16 + s, 16, stride=32), :] = imag
        for h in range(2):
            theirs = slabs.at[p, :, h, 1 - core]
            send(theirs, core_in.at[h, p], core_s.at[h, p], core_r.at[h, p], sibling)

    def fill(step, carry):
        rows = (step % 8) * 128 + iota((128, 256), 0)
        block = order[:, pl.ds(pl.multiple_of((step // 8) * 128, 128), 128)]
        lane_row = jnp.concatenate([block * 2, block * 2 + 1], axis=1)
        perm[step // 8, pl.ds(pl.multiple_of((step % 8) * 128, 128), 128), :] = as_bf16(rows == lane_row)
        return carry

    for h in range(2):
        for p in range(POLARS):
            arrived(core_in.at[h, p], core_s.at[h, p], core_r.at[h, p])
            for d in (1, 2, 3):
                to = (x + d) % 4
                x_out[h, p, d - 1] = slabs[p, to, h, core] + core_in[h, p, to]
                send(
                    x_out.at[h, p, d - 1], x_in.at[h, p, d - 1],
                    x_s.at[h, p, d - 1], x_r.at[h, p, d - 1], x_peer[d - 1],
                )
        lax.fori_loop(h * 16, h * 16 + 16, fill, 0)
        for p in range(POLARS):
            total = slabs[p, x, h, core] + core_in[h, p, x]
            for d in (1, 2, 3):
                arrived(x_in.at[h, p, d - 1], x_s.at[h, p, d - 1], x_r.at[h, p, d - 1])
                total += x_in[h, p, d - 1]

            @pl.when(zi == h)
            def _():
                z_own[p] = total

            @pl.when(zi != h)
            def _():
                z_out[p] = total.astype(BF16)

        if h == 1:

            @pl.when(zi == 0)
            def _():
                pl.semaphore_wait(ready, 4)
                for partner in far_peer:
                    pl.semaphore_signal(ready, inc=1, device_id=partner, device_id_type=MESH)

            @pl.when(zi == 1)
            def _():
                pl.semaphore_wait(ready, 4)

        @pl.when(zi == h)
        def _():
            for e in range(4):
                to_z(0, e).start()

        @pl.when(zi != h)
        def _():
            for e in range(4):
                to_z(1, e).start()

    for d in (1, 2, 3, 0):
        source = (zh - d + 4) % 4
        arrived(near_in.at[source], z_s.at[0, d], z_r.at[0, source])
        arrived(far_in.at[source], z_s.at[1, d], z_r.at[1, source])
        held[source, 1 - par, y] = (near_in[source] + far_in[source].astype(F32)).astype(BF16)
        mine = held.at[source, 1 - par, y]
        send(mine, mine, y_s.at[d, 6], y_r.at[d, 1 - par, 0], pair_peer)
        for j, (_, step) in enumerate(y_steps):
            send(mine, mine, y_s.at[d, j], y_r.at[d, 1 - par, step], y_peer[j])

    for d in (1, 2, 3, 0):
        source = (zh - d + 4) % 4
        arrived(held.at[source, par, y], y_s.at[d, 6], y_r.at[d, par, 0])
        for j, (e, step) in enumerate(y_steps):
            arrived(held.at[source, 1 - e, (y - step + 4) % 4], y_s.at[d, j], y_r.at[d, 1 - e, step])
        right = jnp.concatenate(
            [
                jnp.concatenate([held[source, :, :, p, k].reshape(128, SPECTRA) for p in range(POLARS)], axis=0)
                for k in range(2)
            ],
            axis=1,
        )
        for step in range(4):
            rows = pl.ds(step * 256, 256)
            got = jnp.dot(perm[source, rows, :], right, preferred_element_type=F32)
            if d == 1:
                summed[rows, :] = got
            elif d > 0:
                summed[rows, :] += got
            else:
                ordered[rows, :] = (summed[rows, :] + got).astype(BF16)
    mine = ordered[pl.ds(pl.multiple_of(group * 32, 32), 32), :]
    turned = jnp.concatenate([mine[:, SPECTRA:], -mine[:, :SPECTRA]], axis=1)
    left = jnp.concatenate([mine, turned], axis=0)
    for step in range(4):
        block = ordered[pl.ds(step * 256, 256), :]
        seen = lax.dot_general(left, block, (((1,), (1,)), ((), ())), preferred_element_type=F32)
        seen = seen * (1.0 / SPECTRA)
        out[0, :, pl.ds(step * 256, 256)] = seen[:32]
        out[1, :, pl.ds(step * 256, 256)] = seen[32:]
    for copy in started:
        copy.wait_send()
    for far in range(2):
        for e in range(4):
            to_z(far, e).wait_send()


def body(voltages, weights, antenna_slot_index, station_order):
    wt = jnp.transpose(weights, (0, 1, 3, 4, 2)).reshape(1024, ANTENNAS)
    vmem = pl.BlockSpec(memory_space=pltpu.VMEM)
    hbm = pl.BlockSpec(memory_space=pltpu.HBM)
    sem = pltpu.SemaphoreType.DMA
    out = pl.pallas_call(
        kernel,
        out_shape=jax.ShapeDtypeStruct((2, 32, 1024), F32),
        in_specs=[hbm, hbm, hbm, hbm],
        out_specs=vmem,
        scratch_shapes=[
            pltpu.VMEM((STATIONS, SLOTS), I32),
            pltpu.VMEM((1, 512), I32),
            pltpu.VMEM((2, 2, STATIONS, SLOTS, CHANNELS, SPECTRA), BF16),
            pltpu.VMEM((1024, ANTENNAS), BF16),
            pltpu.VMEM((1024, 256), BF16),
            pltpu.VMEM((1024, SPECTRA), F32),
            pltpu.VMEM((2, 2, 4, 2, STATIONS, SPECTRA), F32),
            pltpu.VMEM((2, 2, 3, 2, STATIONS, SPECTRA), F32),
            pltpu.VMEM((2, 2, 3, 2, STATIONS, SPECTRA), F32),
            pltpu.VMEM((2, 2, STATIONS, SPECTRA), F32),
            pltpu.VMEM((2, 2, STATIONS, SPECTRA), BF16),
            pltpu.VMEM((4, 2, 2, STATIONS, SPECTRA), F32),
            pltpu.VMEM((4, 2, 2, STATIONS, SPECTRA), BF16),
            pltpu.VMEM((4, 2, 4, 2, 2, STATIONS, SPECTRA), BF16),
            pltpu.VMEM((4, 1024, 256), BF16),
            pltpu.VMEM((1024, 256), F32),
            pltpu.VMEM((1024, 256), BF16),
            sem((2,)), sem((2, 2)), sem,
            sem((2, 2)), sem((2, 2)),
            sem((2, 2, 3)), sem((2, 2, 3)),
            sem((2, 4)), sem((2, 4)), pltpu.SemaphoreType.REGULAR,
            sem((4, 7)), sem((4, 2, 4)),
        ],
        compiler_params=pltpu.CompilerParams(
            collective_id=0, has_side_effects=True, vmem_limit_bytes=54700 * 1024
        ),
    )(voltages, wt, antenna_slot_index, station_order.reshape(1, 512))
    return out[None]


def solution(mesh):
    in_specs = (
        P(None, "sgroup", "tile", None, None, None),
        P(None, "sgroup", None, None, None),
        P("sgroup", "tile"),
        P(),
    )
    out_specs = P("tile", None, "sgroup", None)
    return jax.shard_map(body, mesh=mesh, in_specs=in_specs, out_specs=out_specs, check_vma=False)
```

```python
import functools

import jax
import jax.numpy as jnp
from jax import lax
from jax.experimental import pallas as pl
from jax.experimental.pallas import tpu as pltpu
from jax.sharding import PartitionSpec as P

MESH = pl.DeviceIdType.MESH
F32, BF16, I32 = jnp.float32, jnp.bfloat16, jnp.int32
EARLY, PASSED_AFTER = (1, 2, 3), {3: 1, 0: 2, 4: 3}
STATIONS, SLOTS, POLARS, CHANNELS, SPECTRA, ANTENNAS = 16, 16, 2, 16, 128, 256


def iota(shape, dim):
    return lax.broadcasted_iota(I32, shape, dim)


def as_bf16(mask):
    return jnp.where(mask, 1.0, 0.0).astype(BF16)


def kernel(
    volt, wt, idx_in, order_in, out,
    idx, order, vbuf, wbuf, wexp, part, core_in, x_out, x_in, z_own, z_out, near_in, far_in, held, perm, summed, ordered,
    i_sem, v_sem, w_sem, core_s, core_r, x_s, x_r, z_s, z_r, ready, y_s, y_r,
):
    group, tile = lax.axis_index("sgroup"), lax.axis_index("tile")
    z, y = group // 4, group % 4
    zh, par = z // 2, z % 2
    x, zi, core = tile // 4, (tile // 2) % 2, tile % 2

    def at(g, t):
        return {"sgroup": g, "tile": t}

    sibling = at(group, x * 4 + zi * 2 + (1 - core))
    x_peer = [at(group, ((x + d) % 4) * 4 + zi * 2 + core) for d in (1, 2, 3)]
    z_peer = [
        [at((e * 2 + 1 - par) * 4 + y, x * 4 + half * 2 + core) for e in range(4)] for half in (zi, 1 - zi)
    ]
    near_peer, far_peer = z_peer
    pair_peer = at((zh * 2 + 1 - par) * 4 + y, tile)
    y_steps = [(e, d) for e in (0, 1) for d in (2, 1, 3)]
    y_peer = [at((zh * 2 + e) * 4 + (y + d) % 4, tile) for e, d in y_steps]
    own_y_peer = [at(z * 4 + (y + d) % 4, tile) for d in (2, 1, 3)]

    barrier = pltpu.get_barrier_semaphore()
    partners = [sibling, *x_peer, pair_peer, *y_peer]

    small = [
        pltpu.make_async_copy(idx_in, idx, i_sem.at[0]),
        pltpu.make_async_copy(order_in, order, i_sem.at[1]),
    ]
    for copy in small:
        copy.start()
    w_copy = pltpu.make_async_copy(wt, wbuf, w_sem)
    w_copy.start()
    v_copies = []
    for p in range(POLARS):
        for q in range(2):
            copy = pltpu.make_async_copy(
                volt.at[:, pl.ds(q * 8, 8), :, p], vbuf.at[p, :, pl.ds(q * 8, 8)], v_sem.at[p, q]
            )
            copy.start()
            v_copies.append(copy)

    for partner in partners:
        pl.semaphore_signal(barrier, inc=1, device_id=partner, device_id_type=MESH)

    @pl.when(zi == 0)
    def _():
        for partner in near_peer + far_peer:
            pl.semaphore_signal(barrier, inc=1, device_id=partner, device_id_type=MESH)

    started = []

    def send(src, dst, s, r, device):
        copy = pltpu.make_async_remote_copy(
            src_ref=src, dst_ref=dst, send_sem=s, recv_sem=r, device_id=device, device_id_type=MESH
        )
        copy.start()
        started.append(copy)

    def to_z(far, e):
        return pltpu.make_async_remote_copy(
            src_ref=(z_own, z_out)[far], dst_ref=(near_in, far_in)[far].at[zh], send_sem=z_s.at[far, e],
            recv_sem=z_r.at[far, zh], device_id=z_peer[far][e], device_id_type=MESH,
        )

    def arrived(dst, s, r):
        pltpu.make_async_remote_copy(
            src_ref=dst, dst_ref=dst, send_sem=s, recv_sem=r, device_id=sibling, device_id_type=MESH
        ).wait_recv()

    for copy in small:
        copy.wait()
    lanes = SLOTS * CHANNELS
    spread = as_bf16(iota((SLOTS, lanes), 0) == iota((SLOTS, lanes), 1) % SLOTS)
    wide = jnp.dot(idx[...].astype(BF16), spread, preferred_element_type=F32)
    own_lane = iota((STATIONS, lanes), 0) == iota((STATIONS, lanes), 1) // SLOTS
    wide = jnp.where(own_lane, wide, 0.0).astype(BF16)
    number = jnp.dot(jnp.ones((ANTENNAS, STATIONS), BF16), wide, preferred_element_type=F32)
    onehot = as_bf16(number == iota((ANTENNAS, lanes), 0).astype(F32))
    unfold = as_bf16(iota((lanes, lanes), 0) % SLOTS == iota((lanes, lanes), 1) // CHANNELS)
    w_copy.wait()

    def pick(step):
        kept = (step % 2) * 8 + iota((256, lanes), 0) // 32 == iota((256, lanes), 1) // SLOTS
        block = wbuf[pl.ds(step * 256, 256), :]
        got = jnp.dot(block, onehot, preferred_element_type=F32)
        got = jnp.where(kept, got, 0.0).astype(BF16)
        got = jnp.dot(got, unfold, preferred_element_type=F32)
        same = iota((256, lanes), 0) % CHANNELS == iota((256, lanes), 1) % CHANNELS
        wexp[pl.ds(step * 256, 256), :] = jnp.where(same, got, 0.0).astype(BF16)

    for step in range(4):
        pick(step)

    pl.semaphore_wait(barrier, len(partners) + 4)

    @pl.when(zi == 1)
    def _():
        for partner in far_peer:
            pl.semaphore_signal(ready, inc=1, device_id=partner, device_id_type=MESH)

    slabs = part.reshape(POLARS, 4, 2, 2, 2, STATIONS, SPECTRA)
    for p in range(POLARS):
        for q in range(2):
            v_copies[p * 2 + q].wait()
            for s in range(q * 8, q * 8 + 8):
                left = jnp.concatenate(
                    [wexp[pl.ds(((k * STATIONS + s) * 2 + p) * 16, 16), :] for k in (0, 1)], axis=0
                )
                right = jnp.concatenate(
                    [vbuf[p, k, s].reshape(lanes, SPECTRA) for k in (0, 1)], axis=1
                )
                both = jnp.dot(left, right, preferred_element_type=F32)
                real = both[:16, :SPECTRA] - both[16:, SPECTRA:]
                imag = both[:16, SPECTRA:] + both[16:, :SPECTRA]
                part[pl.ds(p * 512 + s, 16, stride=32), :] = real
                part[pl.ds(p * 512 + 16 + s, 16, stride=32), :] = imag
        for h in range(2):
            theirs = slabs.at[p, :, h, 1 - core]
            send(theirs, core_in.at[h, p], core_s.at[h, p], core_r.at[h, p], sibling)

    def fill(step, carry):
        rows = (step % 8) * 128 + iota((128, 256), 0)
        block = order[:, pl.ds(pl.multiple_of((step // 8) * 128, 128), 128)]
        lane_row = jnp.concatenate([block * 2, block * 2 + 1], axis=1)
        perm[step // 8, pl.ds(pl.multiple_of((step % 8) * 128, 128), 128), :] = as_bf16(rows == lane_row)
        return carry

    for h in range(2):
        for p in range(POLARS):
            arrived(core_in.at[h, p], core_s.at[h, p], core_r.at[h, p])
            for d in (2, 1, 3):
                to = (x + d) % 4
                x_out[h, p, d - 1] = slabs[p, to, h, core] + core_in[h, p, to]
                send(
                    x_out.at[h, p, d - 1], x_in.at[h, p, d - 1],
                    x_s.at[h, p, d - 1], x_r.at[h, p, d - 1], x_peer[d - 1],
                )
        lax.fori_loop(h * 16, h * 16 + 16, fill, 0)
        if h == 1:

            @pl.when(zi == 1)
            def _():
                for e in (2, 3):
                    to_z(1, e).start()

        for p in range(POLARS):
            total = slabs[p, x, h, core] + core_in[h, p, x]
            for d in (1, 2, 3):
                arrived(x_in.at[h, p, d - 1], x_s.at[h, p, d - 1], x_r.at[h, p, d - 1])
                total += x_in[h, p, d - 1]

            @pl.when(zi == h)
            def _():
                z_own[p] = total

            @pl.when(zi != h)
            def _():
                z_out[p] = total.astype(BF16)

        if h == 1:

            @pl.when(zi == 0)
            def _():
                pl.semaphore_wait(ready, 4)
                for partner in far_peer:
                    pl.semaphore_signal(ready, inc=1, device_id=partner, device_id_type=MESH)

            @pl.when(zi == 1)
            def _():
                pl.semaphore_wait(ready, 4)

        @pl.when(zi == h)
        def _():
            for e in range(4):
                to_z(0, e).start()

        @pl.when(zi != h)
        def _():
            for e in range(2 if h == 0 else 4):
                to_z(1, e).start()

    for d in (1, 2, 3, 0):
        source = (zh - d + 4) % 4
        arrived(near_in.at[source], z_s.at[0, d], z_r.at[0, source])
        arrived(far_in.at[source], z_s.at[1, d], z_r.at[1, source])
        held[source, 1 - par, y] = (near_in[source] + far_in[source].astype(F32)).astype(BF16)
        mine = held.at[source, 1 - par, y]
        send(mine, mine, y_s.at[d, 6], y_r.at[d, 1 - par, 0], pair_peer)
        if d in EARLY:
            for j, step in enumerate((2, 1, 3)):
                send(mine, mine, y_s.at[d, j], y_r.at[d, 1 - par, step], own_y_peer[j])
        else:
            for j, (_, step) in enumerate(y_steps):
                send(mine, mine, y_s.at[d, j], y_r.at[d, 1 - par, step], y_peer[j])
        if d in PASSED_AFTER:
            early = PASSED_AFTER[d]
            other = held.at[(zh - early + 4) % 4, par, y]
            arrived(other, y_s.at[early, 6], y_r.at[early, par, 0])
            for j, step in enumerate((2, 1, 3)):
                send(other, other, y_s.at[early, 3 + j], y_r.at[early, par, step], own_y_peer[j])
    if 3 in EARLY:
        other = held.at[(zh - 3 + 4) % 4, par, y]
        arrived(other, y_s.at[3, 6], y_r.at[3, par, 0])
        for j, step in enumerate((2, 1, 3)):
            send(other, other, y_s.at[3, 3 + j], y_r.at[3, par, step], own_y_peer[j])

    for d in (1, 2, 3, 0):
        source = (zh - d + 4) % 4
        if d not in EARLY:
            arrived(held.at[source, par, y], y_s.at[d, 6], y_r.at[d, par, 0])
        for j, (e, step) in enumerate(y_steps):
            arrived(held.at[source, 1 - e, (y - step + 4) % 4], y_s.at[d, j], y_r.at[d, 1 - e, step])
        right = jnp.concatenate(
            [
                jnp.concatenate([held[source, :, :, p, k].reshape(128, SPECTRA) for p in range(POLARS)], axis=0)
                for k in range(2)
            ],
            axis=1,
        )
        for step in range(4):
            rows = pl.ds(step * 256, 256)
            got = jnp.dot(perm[source, rows, :], right, preferred_element_type=F32)
            if d == 1:
                summed[rows, :] = got
            elif d > 0:
                summed[rows, :] += got
            else:
                ordered[rows, :] = (summed[rows, :] + got).astype(BF16)
    mine = ordered[pl.ds(pl.multiple_of(group * 32, 32), 32), :]
    turned = jnp.concatenate([mine[:, SPECTRA:], -mine[:, :SPECTRA]], axis=1)
    left = jnp.concatenate([mine, turned], axis=0)
    for step in range(4):
        block = ordered[pl.ds(step * 256, 256), :]
        seen = lax.dot_general(left, block, (((1,), (1,)), ((), ())), preferred_element_type=F32)
        seen = seen * (1.0 / SPECTRA)
        out[0, :, pl.ds(step * 256, 256)] = seen[:32]
        out[1, :, pl.ds(step * 256, 256)] = seen[32:]
    for copy in started:
        copy.wait_send()
    for far in range(2):
        for e in range(4):
            to_z(far, e).wait_send()


def body(voltages, weights, antenna_slot_index, station_order):
    wt = jnp.transpose(weights, (0, 1, 3, 4, 2)).reshape(1024, ANTENNAS)
    vmem = pl.BlockSpec(memory_space=pltpu.VMEM)
    hbm = pl.BlockSpec(memory_space=pltpu.HBM)
    sem = pltpu.SemaphoreType.DMA
    out = pl.pallas_call(
        kernel,
        out_shape=pltpu.VMEM((2, 32, 1024), F32),
        in_specs=[hbm, hbm, hbm, hbm],
        out_specs=vmem,
        scratch_shapes=[
            pltpu.VMEM((STATIONS, SLOTS), I32),
            pltpu.VMEM((1, 512), I32),
            pltpu.VMEM((2, 2, STATIONS, SLOTS, CHANNELS, SPECTRA), BF16),
            pltpu.VMEM((1024, ANTENNAS), BF16),
            pltpu.VMEM((1024, 256), BF16),
            pltpu.VMEM((1024, SPECTRA), F32),
            pltpu.VMEM((2, 2, 4, 2, STATIONS, SPECTRA), F32),
            pltpu.VMEM((2, 2, 3, 2, STATIONS, SPECTRA), F32),
            pltpu.VMEM((2, 2, 3, 2, STATIONS, SPECTRA), F32),
            pltpu.VMEM((2, 2, STATIONS, SPECTRA), F32),
            pltpu.VMEM((2, 2, STATIONS, SPECTRA), BF16),
            pltpu.VMEM((4, 2, 2, STATIONS, SPECTRA), F32),
            pltpu.VMEM((4, 2, 2, STATIONS, SPECTRA), BF16),
            pltpu.VMEM((4, 2, 4, 2, 2, STATIONS, SPECTRA), BF16),
            pltpu.VMEM((4, 1024, 256), BF16),
            pltpu.VMEM((1024, 256), F32),
            pltpu.VMEM((1024, 256), BF16),
            sem((2,)), sem((2, 2)), sem,
            sem((2, 2)), sem((2, 2)),
            sem((2, 2, 3)), sem((2, 2, 3)),
            sem((2, 4)), sem((2, 4)), pltpu.SemaphoreType.REGULAR,
            sem((4, 7)), sem((4, 2, 4)),
        ],
        compiler_params=pltpu.CompilerParams(
            collective_id=0, has_side_effects=True, vmem_limit_bytes=56 * 2**20
        ),
    )(voltages, wt, antenna_slot_index, station_order.reshape(1, 512))
    return out[None]


def solution(mesh):
    in_specs = (
        P(None, "sgroup", "tile", None, None, None),
        P(None, "sgroup", None, None, None),
        P("sgroup", "tile"),
        P(),
    )
    out_specs = P("tile", None, "sgroup", None)
    return jax.shard_map(body, mesh=mesh, in_specs=in_specs, out_specs=out_specs, check_vma=False)
```

```python
import functools

import jax
import jax.numpy as jnp
from jax import lax
from jax.experimental import pallas as pl
from jax.experimental.pallas import tpu as pltpu
from jax.sharding import PartitionSpec as P

MESH = pl.DeviceIdType.MESH
F32, BF16, I32 = jnp.float32, jnp.bfloat16, jnp.int32
EARLY, PASSED_AFTER = (1, 2, 3), {3: 1, 0: 2, 4: 3}
STATIONS, SLOTS, POLARS, CHANNELS, SPECTRA, ANTENNAS = 16, 16, 2, 16, 128, 256


def iota(shape, dim):
    return lax.broadcasted_iota(I32, shape, dim)


def as_bf16(mask):
    return jnp.where(mask, 1.0, 0.0).astype(BF16)


def kernel(
    volt, wt, idx_in, order_in, out,
    idx, order, vbuf, wbuf, wexp, part, x_wide, x_out, x_in, z_own, z_out, near_in, far_in, held, perm, summed, ordered,
    i_sem, v_sem, w_sem, x_s, x_r, z_s, z_r, ready, y_s, y_r,
):
    group, tile = lax.axis_index("sgroup"), lax.axis_index("tile")
    z, y = group // 4, group % 4
    zh, par = z // 2, z % 2
    x, zi, core = tile // 4, (tile // 2) % 2, tile % 2

    def at(g, t):
        return {"sgroup": g, "tile": t}

    x_steps = [(0, 1), (1, 0), (3, 0), (2, 0), (2, 1), (1, 1), (3, 1)]
    cores = (core, 1 - core)
    x_peer = [at(group, ((x + d) % 4) * 4 + zi * 2 + cores[c]) for d, c in x_steps]
    z_peer = [
        [at((e * 2 + 1 - par) * 4 + y, x * 4 + half * 2 + core) for e in range(4)] for half in (zi, 1 - zi)
    ]
    near_peer, far_peer = z_peer
    pair_peer = at((zh * 2 + 1 - par) * 4 + y, tile)
    y_steps = [(e, d) for e in (0, 1) for d in (2, 1, 3)]
    y_peer = [at((zh * 2 + e) * 4 + (y + d) % 4, tile) for e, d in y_steps]
    own_y_peer = [at(z * 4 + (y + d) % 4, tile) for d in (2, 1, 3)]

    barrier = pltpu.get_barrier_semaphore()
    partners = [*x_peer, pair_peer, *y_peer]

    small = [
        pltpu.make_async_copy(idx_in, idx, i_sem.at[0]),
        pltpu.make_async_copy(order_in, order, i_sem.at[1]),
    ]
    for copy in small:
        copy.start()
    w_copy = pltpu.make_async_copy(wt, wbuf, w_sem)
    w_copy.start()
    v_copies = []
    for p in range(POLARS):
        for q in range(2):
            copy = pltpu.make_async_copy(
                volt.at[:, pl.ds(q * 8, 8), :, p], vbuf.at[p, :, pl.ds(q * 8, 8)], v_sem.at[p, q]
            )
            copy.start()
            v_copies.append(copy)

    for partner in partners:
        pl.semaphore_signal(barrier, inc=1, device_id=partner, device_id_type=MESH)

    @pl.when(zi == 0)
    def _():
        for partner in near_peer + far_peer:
            pl.semaphore_signal(barrier, inc=1, device_id=partner, device_id_type=MESH)

    started = []

    def send(src, dst, s, r, device):
        copy = pltpu.make_async_remote_copy(
            src_ref=src, dst_ref=dst, send_sem=s, recv_sem=r, device_id=device, device_id_type=MESH
        )
        copy.start()
        started.append(copy)

    def to_z(far, e):
        return pltpu.make_async_remote_copy(
            src_ref=(z_own, z_out)[far], dst_ref=(near_in, far_in)[far].at[zh], send_sem=z_s.at[far, e],
            recv_sem=z_r.at[far, zh], device_id=z_peer[far][e], device_id_type=MESH,
        )

    def arrived(dst, s, r):
        pltpu.make_async_remote_copy(
            src_ref=dst, dst_ref=dst, send_sem=s, recv_sem=r, device_id=pair_peer, device_id_type=MESH
        ).wait_recv()

    for copy in small:
        copy.wait()
    lanes = SLOTS * CHANNELS
    spread = as_bf16(iota((SLOTS, lanes), 0) == iota((SLOTS, lanes), 1) % SLOTS)
    wide = jnp.dot(idx[...].astype(BF16), spread, preferred_element_type=F32)
    own_lane = iota((STATIONS, lanes), 0) == iota((STATIONS, lanes), 1) // SLOTS
    wide = jnp.where(own_lane, wide, 0.0).astype(BF16)
    number = jnp.dot(jnp.ones((ANTENNAS, STATIONS), BF16), wide, preferred_element_type=F32)
    onehot = as_bf16(number == iota((ANTENNAS, lanes), 0).astype(F32))
    unfold = as_bf16(iota((lanes, lanes), 0) % SLOTS == iota((lanes, lanes), 1) // CHANNELS)
    w_copy.wait()

    def pick(step):
        kept = (step % 2) * 8 + iota((256, lanes), 0) // 32 == iota((256, lanes), 1) // SLOTS
        block = wbuf[pl.ds(step * 256, 256), :]
        got = jnp.dot(block, onehot, preferred_element_type=F32)
        got = jnp.where(kept, got, 0.0).astype(BF16)
        got = jnp.dot(got, unfold, preferred_element_type=F32)
        same = iota((256, lanes), 0) % CHANNELS == iota((256, lanes), 1) % CHANNELS
        wexp[pl.ds(step * 256, 256), :] = jnp.where(same, got, 0.0).astype(BF16)

    for step in range(4):
        pick(step)

    pl.semaphore_wait(barrier, len(partners) + 4)

    @pl.when(zi == 1)
    def _():
        for partner in far_peer:
            pl.semaphore_signal(ready, inc=1, device_id=partner, device_id_type=MESH)

    slabs = part.reshape(POLARS, 4, 2, 2, 2, STATIONS, SPECTRA)
    def x_slot(h, p, j):
        return x_wide.at[h, p, j] if j < 3 else x_in.at[h, p, j - 3]

    def to_x(h, p):
        for j, (d, c) in enumerate(x_steps):
            source = slabs.at[p, (x + d) % 4, h, cores[c]]
            if j >= 3:
                x_out[h, p, j - 3] = source[...].astype(BF16)
                source = x_out.at[h, p, j - 3]
            send(source, x_slot(h, p, j), x_s.at[h, p, j], x_r.at[h, p, j], x_peer[j])

    for p in range(POLARS):
        for q in range(2):
            v_copies[p * 2 + q].wait()
            for s in range(q * 8, q * 8 + 8):
                left = jnp.concatenate(
                    [wexp[pl.ds(((k * STATIONS + s) * 2 + p) * 16, 16), :] for k in (0, 1)], axis=0
                )
                right = jnp.concatenate(
                    [vbuf[p, k, s].reshape(lanes, SPECTRA) for k in (0, 1)], axis=1
                )
                both = jnp.dot(left, right, preferred_element_type=F32)
                real = both[:16, :SPECTRA] - both[16:, SPECTRA:]
                imag = both[:16, SPECTRA:] + both[16:, :SPECTRA]
                part[pl.ds(p * 512 + s, 16, stride=32), :] = real
                part[pl.ds(p * 512 + 16 + s, 16, stride=32), :] = imag
        to_x(0, p)

    def fill(step, carry):
        rows = (step % 8) * 128 + iota((128, 256), 0)
        block = order[:, pl.ds(pl.multiple_of((step // 8) * 128, 128), 128)]
        lane_row = jnp.concatenate([block * 2, block * 2 + 1], axis=1)
        perm[step // 8, pl.ds(pl.multiple_of((step % 8) * 128, 128), 128), :] = as_bf16(rows == lane_row)
        return carry

    for h in range(2):
        if h == 0:
            lax.fori_loop(0, 32, fill, 0)
            for p in range(POLARS):
                to_x(1, p)
        if h == 1:

            @pl.when(zi == 1)
            def _():
                for e in (2, 3):
                    to_z(1, e).start()

        for p in range(POLARS):
            total = slabs[p, x, h, core]
            for j in range(7):
                arrived(x_slot(h, p, j), x_s.at[h, p, j], x_r.at[h, p, j])
                total += x_slot(h, p, j)[...].astype(F32)

            @pl.when(zi == h)
            def _():
                z_own[p] = total

            @pl.when(zi != h)
            def _():
                z_out[p] = total.astype(BF16)

        if h == 1:

            @pl.when(zi == 0)
            def _():
                pl.semaphore_wait(ready, 4)
                for partner in far_peer:
                    pl.semaphore_signal(ready, inc=1, device_id=partner, device_id_type=MESH)

            @pl.when(zi == 1)
            def _():
                pl.semaphore_wait(ready, 4)

        @pl.when(zi == h)
        def _():
            for e in range(4):
                to_z(0, e).start()

        @pl.when(zi != h)
        def _():
            for e in range(2 if h == 0 else 4):
                to_z(1, e).start()

    for d in (1, 2, 3, 0):
        source = (zh - d + 4) % 4
        arrived(near_in.at[source], z_s.at[0, d], z_r.at[0, source])
        arrived(far_in.at[source], z_s.at[1, d], z_r.at[1, source])
        held[source, 1 - par, y] = (near_in[source] + far_in[source].astype(F32)).astype(BF16)
        mine = held.at[source, 1 - par, y]
        send(mine, mine, y_s.at[d, 6], y_r.at[d, 1 - par, 0], pair_peer)
        if d in EARLY:
            for j, step in enumerate((2, 1, 3)):
                send(mine, mine, y_s.at[d, j], y_r.at[d, 1 - par, step], own_y_peer[j])
        else:
            for j, (_, step) in enumerate(y_steps):
                send(mine, mine, y_s.at[d, j], y_r.at[d, 1 - par, step], y_peer[j])
        if d in PASSED_AFTER:
            early = PASSED_AFTER[d]
            other = held.at[(zh - early + 4) % 4, par, y]
            arrived(other, y_s.at[early, 6], y_r.at[early, par, 0])
            for j, step in enumerate((2, 1, 3)):
                send(other, other, y_s.at[early, 3 + j], y_r.at[early, par, step], own_y_peer[j])
    if 3 in EARLY:
        other = held.at[(zh - 3 + 4) % 4, par, y]
        arrived(other, y_s.at[3, 6], y_r.at[3, par, 0])
        for j, step in enumerate((2, 1, 3)):
            send(other, other, y_s.at[3, 3 + j], y_r.at[3, par, step], own_y_peer[j])

    for d in (1, 2, 0, 3):
        source = (zh - d + 4) % 4
        if d not in EARLY:
            arrived(held.at[source, par, y], y_s.at[d, 6], y_r.at[d, par, 0])
        for j, (e, step) in enumerate(y_steps):
            arrived(held.at[source, 1 - e, (y - step + 4) % 4], y_s.at[d, j], y_r.at[d, 1 - e, step])
        right = jnp.concatenate(
            [
                jnp.concatenate([held[source, :, :, p, k].reshape(128, SPECTRA) for p in range(POLARS)], axis=0)
                for k in range(2)
            ],
            axis=1,
        )
        for step in range(4):
            rows = pl.ds(step * 256, 256)
            got = jnp.dot(perm[source, rows, :], right, preferred_element_type=F32)
            if d == 1:
                summed[rows, :] = got
            elif d != 3:
                summed[rows, :] += got
            else:
                ordered[rows, :] = (summed[rows, :] + got).astype(BF16)
    mine = ordered[pl.ds(pl.multiple_of(group * 32, 32), 32), :]
    turned = jnp.concatenate([mine[:, SPECTRA:], -mine[:, :SPECTRA]], axis=1)
    left = jnp.concatenate([mine, turned], axis=0)
    for step in range(4):
        block = ordered[pl.ds(step * 256, 256), :]
        seen = lax.dot_general(left, block, (((1,), (1,)), ((), ())), preferred_element_type=F32)
        seen = seen * (1.0 / SPECTRA)
        out[0, :, pl.ds(step * 256, 256)] = seen[:32]
        out[1, :, pl.ds(step * 256, 256)] = seen[32:]
    for copy in started:
        copy.wait_send()
    for far in range(2):
        for e in range(4):
            to_z(far, e).wait_send()


def body(voltages, weights, antenna_slot_index, station_order):
    wt = jnp.transpose(weights, (0, 1, 3, 4, 2)).reshape(1024, ANTENNAS)
    vmem = pl.BlockSpec(memory_space=pltpu.VMEM)
    hbm = pl.BlockSpec(memory_space=pltpu.HBM)
    sem = pltpu.SemaphoreType.DMA
    out = pl.pallas_call(
        kernel,
        out_shape=pltpu.VMEM((2, 32, 1024), F32),
        in_specs=[hbm, hbm, hbm, hbm],
        out_specs=vmem,
        scratch_shapes=[
            pltpu.VMEM((STATIONS, SLOTS), I32),
            pltpu.VMEM((1, 512), I32),
            pltpu.VMEM((2, 2, STATIONS, SLOTS, CHANNELS, SPECTRA), BF16),
            pltpu.VMEM((1024, ANTENNAS), BF16),
            pltpu.VMEM((1024, 256), BF16),
            pltpu.VMEM((1024, SPECTRA), F32),
            pltpu.VMEM((2, 2, 3, 2, STATIONS, SPECTRA), F32),
            pltpu.VMEM((2, 2, 4, 2, STATIONS, SPECTRA), BF16),
            pltpu.VMEM((2, 2, 4, 2, STATIONS, SPECTRA), BF16),
            pltpu.VMEM((2, 2, STATIONS, SPECTRA), F32),
            pltpu.VMEM((2, 2, STATIONS, SPECTRA), BF16),
            pltpu.VMEM((4, 2, 2, STATIONS, SPECTRA), F32),
            pltpu.VMEM((4, 2, 2, STATIONS, SPECTRA), BF16),
            pltpu.VMEM((4, 2, 4, 2, 2, STATIONS, SPECTRA), BF16),
            pltpu.VMEM((4, 1024, 256), BF16),
            pltpu.VMEM((1024, 256), F32),
            pltpu.VMEM((1024, 256), BF16),
            sem((2,)), sem((2, 2)), sem,
            sem((2, 2, 7)), sem((2, 2, 7)),
            sem((2, 4)), sem((2, 4)), pltpu.SemaphoreType.REGULAR,
            sem((4, 7)), sem((4, 2, 4)),
        ],
        compiler_params=pltpu.CompilerParams(
            collective_id=0, has_side_effects=True, vmem_limit_bytes=56 * 2**20
        ),
    )(voltages, wt, antenna_slot_index, station_order.reshape(1, 512))
    return out[None]


def solution(mesh):
    in_specs = (
        P(None, "sgroup", "tile", None, None, None),
        P(None, "sgroup", None, None, None),
        P("sgroup", "tile"),
        P(),
    )
    out_specs = P("tile", None, "sgroup", None)
    return jax.shard_map(body, mesh=mesh, in_specs=in_specs, out_specs=out_specs, check_vma=False)
```

```python
import functools

import jax
import jax.numpy as jnp
from jax import lax
from jax.experimental import pallas as pl
from jax.experimental.pallas import tpu as pltpu
from jax.sharding import PartitionSpec as P

MESH = pl.DeviceIdType.MESH
F32, BF16, I32 = jnp.float32, jnp.bfloat16, jnp.int32
EARLY, PASSED_AFTER = (1, 2, 3), {3: 1, 0: 2, 4: 3}
STATIONS, SLOTS, POLARS, CHANNELS, SPECTRA, ANTENNAS = 16, 16, 2, 16, 128, 256


def iota(shape, dim):
    return lax.broadcasted_iota(I32, shape, dim)


def as_bf16(mask):
    return jnp.where(mask, 1.0, 0.0).astype(BF16)


def kernel(
    volt, wt, idx_in, order_in, out,
    idx, order, vbuf, wbuf, wexp, part, x_wide, x_out, x_in, z_own, z_out, near_in, far_in, held, perm, summed, ordered,
    i_sem, v_sem, w_sem, x_s, x_r, z_s, z_r, ready, y_s, y_r,
):
    group, tile = lax.axis_index("sgroup"), lax.axis_index("tile")
    z, y = group // 4, group % 4
    zh, par = z // 2, z % 2
    x, zi, core = tile // 4, (tile // 2) % 2, tile % 2

    def at(g, t):
        return {"sgroup": g, "tile": t}

    x_steps = [(0, 1), (1, 0), (3, 0), (2, 0), (2, 1), (1, 1), (3, 1)]
    cores = (core, 1 - core)
    x_peer = [at(group, ((x + d) % 4) * 4 + zi * 2 + cores[c]) for d, c in x_steps]
    z_peer = [
        [at((e * 2 + 1 - par) * 4 + y, x * 4 + half * 2 + core) for e in range(4)] for half in (zi, 1 - zi)
    ]
    near_peer, far_peer = z_peer
    pair_peer = at((zh * 2 + 1 - par) * 4 + y, tile)
    y_steps = [(e, d) for e in (0, 1) for d in (2, 1, 3)]
    y_peer = [at((zh * 2 + e) * 4 + (y + d) % 4, tile) for e, d in y_steps]
    own_y_peer = [at(z * 4 + (y + d) % 4, tile) for d in (2, 1, 3)]

    barrier = pltpu.get_barrier_semaphore()
    partners = [*x_peer, pair_peer, *y_peer]

    small = [
        pltpu.make_async_copy(idx_in, idx, i_sem.at[0]),
        pltpu.make_async_copy(order_in, order, i_sem.at[1]),
    ]
    for copy in small:
        copy.start()
    w_copy = pltpu.make_async_copy(wt, wbuf, w_sem)
    w_copy.start()
    v_copies = []
    for p in range(POLARS):
        copy = pltpu.make_async_copy(volt.at[:, :, :, p], vbuf.at[p], v_sem.at[p])
        copy.start()
        v_copies.append(copy)

    for partner in partners:
        pl.semaphore_signal(barrier, inc=1, device_id=partner, device_id_type=MESH)

    @pl.when(zi == 0)
    def _():
        for partner in near_peer + far_peer:
            pl.semaphore_signal(barrier, inc=1, device_id=partner, device_id_type=MESH)

    started = []

    def send(src, dst, s, r, device):
        copy = pltpu.make_async_remote_copy(
            src_ref=src, dst_ref=dst, send_sem=s, recv_sem=r, device_id=device, device_id_type=MESH
        )
        copy.start()
        started.append(copy)

    def to_z(far, e):
        return pltpu.make_async_remote_copy(
            src_ref=(z_own, z_out)[far], dst_ref=(near_in, far_in)[far].at[zh], send_sem=z_s.at[far, e],
            recv_sem=z_r.at[far, zh], device_id=z_peer[far][e], device_id_type=MESH,
        )

    def arrived(dst, s, r):
        pltpu.make_async_remote_copy(
            src_ref=dst, dst_ref=dst, send_sem=s, recv_sem=r, device_id=pair_peer, device_id_type=MESH
        ).wait_recv()

    for copy in small:
        copy.wait()
    lanes = SLOTS * CHANNELS
    spread = as_bf16(iota((SLOTS, lanes), 0) == iota((SLOTS, lanes), 1) % SLOTS)
    wide = jnp.dot(idx[...].astype(BF16), spread, preferred_element_type=F32)
    own_lane = iota((STATIONS, lanes), 0) == iota((STATIONS, lanes), 1) // SLOTS
    wide = jnp.where(own_lane, wide, 0.0).astype(BF16)
    number = jnp.dot(jnp.ones((ANTENNAS, STATIONS), BF16), wide, preferred_element_type=F32)
    onehot = as_bf16(number == iota((ANTENNAS, lanes), 0).astype(F32))
    unfold = as_bf16(iota((lanes, lanes), 0) % SLOTS == iota((lanes, lanes), 1) // CHANNELS)
    w_copy.wait()

    def pick(step):
        kept = (step % 2) * 8 + iota((256, lanes), 0) // 32 == iota((256, lanes), 1) // SLOTS
        block = wbuf[pl.ds(step * 256, 256), :]
        got = jnp.dot(block, onehot, preferred_element_type=F32)
        got = jnp.where(kept, got, 0.0).astype(BF16)
        got = jnp.dot(got, unfold, preferred_element_type=F32)
        same = iota((256, lanes), 0) % CHANNELS == iota((256, lanes), 1) % CHANNELS
        wexp[pl.ds(step * 256, 256), :] = jnp.where(same, got, 0.0).astype(BF16)

    for step in range(4):
        pick(step)

    pl.semaphore_wait(barrier, len(partners) + 4)

    @pl.when(zi == 1)
    def _():
        for partner in far_peer:
            pl.semaphore_signal(ready, inc=1, device_id=partner, device_id_type=MESH)

    slabs = part.reshape(POLARS, 4, 2, 2, 2, STATIONS, SPECTRA)
    def x_slot(h, p, j):
        return x_wide.at[h, p, j] if j < 3 else x_in.at[h, p, j - 3]

    def to_x(h, p):
        for j, (d, c) in enumerate(x_steps):
            source = slabs.at[p, (x + d) % 4, h, cores[c]]
            if j >= 3:
                x_out[h, p, j - 3] = source[...].astype(BF16)
                source = x_out.at[h, p, j - 3]
            send(source, x_slot(h, p, j), x_s.at[h, p, j], x_r.at[h, p, j], x_peer[j])

    for p in range(POLARS):
        v_copies[p].wait()
        for s in range(STATIONS):
            left = jnp.concatenate(
                [wexp[pl.ds(((k * STATIONS + s) * 2 + p) * 16, 16), :] for k in (0, 1)], axis=0
            )
            right = jnp.concatenate(
                [vbuf[p, k, s].reshape(lanes, SPECTRA) for k in (0, 1)], axis=1
            )
            both = jnp.dot(left, right, preferred_element_type=F32)
            real = both[:16, :SPECTRA] - both[16:, SPECTRA:]
            imag = both[:16, SPECTRA:] + both[16:, :SPECTRA]
            part[pl.ds(p * 512 + s, 16, stride=32), :] = real
            part[pl.ds(p * 512 + 16 + s, 16, stride=32), :] = imag
        to_x(0, p)

    def fill(step, carry):
        rows = (step % 8) * 128 + iota((128, 256), 0)
        block = order[:, pl.ds(pl.multiple_of((step // 8) * 128, 128), 128)]
        lane_row = jnp.concatenate([block * 2, block * 2 + 1], axis=1)
        perm[step // 8, pl.ds(pl.multiple_of((step % 8) * 128, 128), 128), :] = as_bf16(rows == lane_row)
        return carry

    for h in range(2):
        if h == 0:
            lax.fori_loop(0, 32, fill, 0)
            for p in range(POLARS):
                to_x(1, p)
        if h == 1:

            @pl.when(zi == 1)
            def _():
                for e in (2, 3):
                    to_z(1, e).start()

        for p in range(POLARS):
            total = slabs[p, x, h, core]
            for j in range(7):
                arrived(x_slot(h, p, j), x_s.at[h, p, j], x_r.at[h, p, j])
                total += x_slot(h, p, j)[...].astype(F32)

            @pl.when(zi == h)
            def _():
                z_own[p] = total

            @pl.when(zi != h)
            def _():
                z_out[p] = total.astype(BF16)

        if h == 1:

            @pl.when(zi == 0)
            def _():
                pl.semaphore_wait(ready, 4)
                for partner in far_peer:
                    pl.semaphore_signal(ready, inc=1, device_id=partner, device_id_type=MESH)

            @pl.when(zi == 1)
            def _():
                pl.semaphore_wait(ready, 4)

        @pl.when(zi == h)
        def _():
            for e in range(4):
                to_z(0, e).start()

        @pl.when(zi != h)
        def _():
            for e in range(2 if h == 0 else 4):
                to_z(1, e).start()

    for d in (1, 2, 3, 0):
        source = (zh - d + 4) % 4
        arrived(near_in.at[source], z_s.at[0, d], z_r.at[0, source])
        arrived(far_in.at[source], z_s.at[1, d], z_r.at[1, source])
        held[source, 1 - par, y] = (near_in[source] + far_in[source].astype(F32)).astype(BF16)
        mine = held.at[source, 1 - par, y]
        send(mine, mine, y_s.at[d, 6], y_r.at[d, 1 - par, 0], pair_peer)
        if d in EARLY:
            for j, step in enumerate((2, 1, 3)):
                send(mine, mine, y_s.at[d, j], y_r.at[d, 1 - par, step], own_y_peer[j])
        else:
            for j, (_, step) in enumerate(y_steps):
                send(mine, mine, y_s.at[d, j], y_r.at[d, 1 - par, step], y_peer[j])
        if d in PASSED_AFTER:
            early = PASSED_AFTER[d]
            other = held.at[(zh - early + 4) % 4, par, y]
            arrived(other, y_s.at[early, 6], y_r.at[early, par, 0])
            for j, step in enumerate((2, 1, 3)):
                send(other, other, y_s.at[early, 3 + j], y_r.at[early, par, step], own_y_peer[j])
    if 3 in EARLY:
        other = held.at[(zh - 3 + 4) % 4, par, y]
        arrived(other, y_s.at[3, 6], y_r.at[3, par, 0])
        for j, step in enumerate((2, 1, 3)):
            send(other, other, y_s.at[3, 3 + j], y_r.at[3, par, step], own_y_peer[j])

    for d in (1, 2, 0, 3):
        source = (zh - d + 4) % 4
        if d not in EARLY:
            arrived(held.at[source, par, y], y_s.at[d, 6], y_r.at[d, par, 0])
        for j, (e, step) in enumerate(y_steps):
            arrived(held.at[source, 1 - e, (y - step + 4) % 4], y_s.at[d, j], y_r.at[d, 1 - e, step])
        right = jnp.concatenate(
            [
                jnp.concatenate([held[source, :, :, p, k].reshape(128, SPECTRA) for p in range(POLARS)], axis=0)
                for k in range(2)
            ],
            axis=1,
        )
        for step in range(4):
            rows = pl.ds(step * 256, 256)
            got = jnp.dot(perm[source, rows, :], right, preferred_element_type=F32)
            if d == 1:
                summed[rows, :] = got
            elif d != 3:
                summed[rows, :] += got
            else:
                ordered[rows, :] = (summed[rows, :] + got).astype(BF16)
    mine = ordered[pl.ds(pl.multiple_of(group * 32, 32), 32), :]
    turned = jnp.concatenate([mine[:, SPECTRA:], -mine[:, :SPECTRA]], axis=1)
    left = jnp.concatenate([mine, turned], axis=0)
    for step in range(4):
        block = ordered[pl.ds(step * 256, 256), :]
        seen = lax.dot_general(left, block, (((1,), (1,)), ((), ())), preferred_element_type=F32)
        seen = seen * (1.0 / SPECTRA)
        out[0, :, pl.ds(step * 256, 256)] = seen[:32]
        out[1, :, pl.ds(step * 256, 256)] = seen[32:]
    for copy in started:
        copy.wait_send()
    for far in range(2):
        for e in range(4):
            to_z(far, e).wait_send()


def body(voltages, weights, antenna_slot_index, station_order):
    wt = jnp.transpose(weights, (0, 1, 3, 4, 2)).reshape(1024, ANTENNAS)
    vmem = pl.BlockSpec(memory_space=pltpu.VMEM)
    hbm = pl.BlockSpec(memory_space=pltpu.HBM)
    sem = pltpu.SemaphoreType.DMA
    out = pl.pallas_call(
        kernel,
        out_shape=pltpu.VMEM((2, 32, 1024), F32),
        in_specs=[hbm, hbm, hbm, hbm],
        out_specs=vmem,
        scratch_shapes=[
            pltpu.VMEM((STATIONS, SLOTS), I32),
            pltpu.VMEM((1, 512), I32),
            pltpu.VMEM((2, 2, STATIONS, SLOTS, CHANNELS, SPECTRA), BF16),
            pltpu.VMEM((1024, ANTENNAS), BF16),
            pltpu.VMEM((1024, 256), BF16),
            pltpu.VMEM((1024, SPECTRA), F32),
            pltpu.VMEM((2, 2, 3, 2, STATIONS, SPECTRA), F32),
            pltpu.VMEM((2, 2, 4, 2, STATIONS, SPECTRA), BF16),
            pltpu.VMEM((2, 2, 4, 2, STATIONS, SPECTRA), BF16),
            pltpu.VMEM((2, 2, STATIONS, SPECTRA), F32),
            pltpu.VMEM((2, 2, STATIONS, SPECTRA), BF16),
            pltpu.VMEM((4, 2, 2, STATIONS, SPECTRA), F32),
            pltpu.VMEM((4, 2, 2, STATIONS, SPECTRA), BF16),
            pltpu.VMEM((4, 2, 4, 2, 2, STATIONS, SPECTRA), BF16),
            pltpu.VMEM((4, 1024, 256), BF16),
            pltpu.VMEM((1024, 256), F32),
            pltpu.VMEM((1024, 256), BF16),
            sem((2,)), sem((2,)), sem,
            sem((2, 2, 7)), sem((2, 2, 7)),
            sem((2, 4)), sem((2, 4)), pltpu.SemaphoreType.REGULAR,
            sem((4, 7)), sem((4, 2, 4)),
        ],
        compiler_params=pltpu.CompilerParams(
            collective_id=0, has_side_effects=True, vmem_limit_bytes=56 * 2**20
        ),
    )(voltages, wt, antenna_slot_index, station_order.reshape(1, 512))
    return out[None]


def solution(mesh):
    in_specs = (
        P(None, "sgroup", "tile", None, None, None),
        P(None, "sgroup", None, None, None),
        P("sgroup", "tile"),
        P(),
    )
    out_specs = P("tile", None, "sgroup", None)
    return jax.shard_map(body, mesh=mesh, in_specs=in_specs, out_specs=out_specs, check_vma=False)
```
